32 devices in a mesh: row: 4 (over z), col: 8 (over y, x, core).
Axes of the slice: x: 2, y: 2, z: 4, core: 2. Of those that a mesh axis runs over, the one named last changes fastest.
Arguments:
- tokens: bfloat16 [256, 8192], P('row', 'col'), may hold values from -6 to 6
- weights: bfloat16 [2, 8192, 28672], P(None, 'col', 'row'), may hold values from -2 to 2
- adapter_in: bfloat16 [2, 64, 8192], P(None, None, 'col'), may hold values from -0.75 to 0.75
- adapter_out: bfloat16 [2, 64, 28672], P(None, None, 'row'), may hold values from -0.3 to 0.3
- magnitude: float32 [2, 28672], P(None, 'row'), may hold values from 0.5 to 2
- hidden_cot: bfloat16 [256, 28672], P('col', 'row'), may hold values from -0.29882812 to 0.29882812
Outputs:
- hidden: bfloat16 [256, 28672], P('col', 'row')
- grad_in: float32 [2, 64, 8192], P(None, None, 'col')
- grad_out: float32 [2, 64, 28672], P(None, None, 'row')
- grad_mag: float32 [2, 28672], P(None, 'row')
The draws below stay inside these ranges and needn't reach their ends.
All inputs are finite; a program needn't handle non-finite values.
Results may differ from the reference program's by a relative error of at most 0.028.
Values may be sent and summed in bfloat16 or wider, within the bound.
No kernel may reach another device: no remote copies, remote signals or barrier semaphores. Data moves between devices by JAX's collectives and lax.ppermute only.
A program may use at most 256 MiB of HBM per device.

```python
import math
import jax
import jax.numpy as jnp
from jax import lax

D = 8192
FF = 28672
R = 64
TOKENS = 256
N_COL = 8


def factor_draws(key):
    key_left, key_right, key_extra = jax.random.split(jax.random.fold_in(key, 29), 3)
    left = jax.random.truncated_normal(key_left, -6.0, 6.0, (2, R, D), jnp.float32)
    right = jax.random.truncated_normal(key_right, -6.0, 6.0, (2, R, FF), jnp.float32)
    extra = jax.random.truncated_normal(key_extra, -6.0, 6.0, (2, R, FF), jnp.float32)
    left_bf = (0.125 * left).astype(jnp.bfloat16)
    right_bf = (0.05 * right).astype(jnp.bfloat16)
    return (left_bf, right_bf, 0.05 * extra)


def draw_adapter_in(key, part):
    return factor_draws(key)[0]


def draw_adapter_out(key, part):
    return factor_draws(key)[1]


def draw_weights(key, part):
    left_bf, right_bf, extra = factor_draws(key)
    key_base, key_rows, key_cols = jax.random.split(jax.random.fold_in(key, 11), 3)
    base = jax.random.truncated_normal(key_base, -4.0, 4.0, (2, D, FF), jnp.float32)
    row_scale = 10.0 ** jax.random.uniform(key_rows, (2, D, 1), jnp.float32)
    col_scale = 10.0 ** jax.random.uniform(key_cols, (2, 1, FF), jnp.float32)
    trend = 3.0 ** (0.5 * jnp.arange(D, dtype=jnp.float32) / D)
    values = base * row_scale * col_scale * trend[None, :, None] / (5.0 * D ** 0.5)
    earlier = extra - 0.8 * right_bf.astype(jnp.float32)
    planted = jnp.einsum('prd,prf->pdf', left_bf.astype(jnp.float32), earlier, precision=lax.Precision.HIGHEST)
    values = jnp.clip(values + planted, -2.0, 2.0)
    return values.astype(jnp.bfloat16)


def shard_levels(stream_key, shape, cuts, least, top_value):
    level, own = 1.0, jax.random.fold_in(stream_key, 6)
    for axis_at, parts in cuts:
        heights = jnp.exp(jax.random.uniform(jax.random.fold_in(own, axis_at), (parts,), jnp.float32, least / len(cuts), top_value / len(cuts)))
        level = level * jnp.repeat(heights, shape[axis_at] // parts).reshape([-1 if axis == axis_at else 1 for axis in range(len(shape))])
    return level


def centred(rng, extent, width, reach, cuts=(), held_as=jnp.bfloat16):
    values = width * jax.random.normal(rng, extent, jnp.float32)
    if cuts:
        values = values * shard_levels(rng, extent, cuts, -0.22, 0.18)
    return jnp.clip(values, -reach, reach).astype(held_as)


def setup_inputs(seed: int = 0) -> dict:
    key_list = jax.random.split(jax.random.key(seed), 7)
    tokens = centred(key_list[0], (TOKENS, D), 1.0, 6.0, ((0, 4), (1, 8)))
    weights = draw_weights(jax.random.fold_in(key_list[6], 71), 0)
    adapter_in = draw_adapter_in(jax.random.fold_in(key_list[6], 71), 0)
    adapter_out = draw_adapter_out(jax.random.fold_in(key_list[6], 71), 0)
    magnitude = jnp.clip(jnp.exp(math.log(2.0) - 1.3862944 * jax.random.uniform(key_list[4], (2, FF), jnp.float32) ** shard_levels(key_list[4], (2, FF), ((1, 4),), -0.2, 0.2)), 0.5, 2.0)
    hidden_cot = centred(key_list[5], (TOKENS, FF), 0.05, 0.29882812, ((0, 8), (1, 4)))
    return dict(tokens=tokens, weights=weights, adapter_in=adapter_in, adapter_out=adapter_out, magnitude=magnitude, hidden_cot=hidden_cot)


EPSILON = 1e-06

def project(tokens, merged):
    width_block = D // N_COL
    blocks_x = tokens.reshape(TOKENS, N_COL, width_block).transpose(1, 0, 2)
    blocks_w = merged.reshape(N_COL, width_block, FF)

    def add_block(running, pair):
        product = jnp.dot(pair[0], pair[1], preferred_element_type=jnp.float32).astype(jnp.bfloat16)
        product = lax.optimization_barrier(product)
        return (running + product.astype(jnp.float32), None)
    running, _ = lax.scan(add_block, jnp.zeros((TOKENS, FF), jnp.float32), (blocks_x, blocks_w))
    return running

def reference(tokens, weights, adapter_in, adapter_out, magnitude, hidden_cot):
    directions = []
    norms = []
    pres = []
    for index in range(2):
        low_rank = jnp.dot(adapter_in[index].T, adapter_out[index], preferred_element_type=jnp.float32)
        direction = weights[index].astype(jnp.float32) + low_rank
        column_norm = jnp.sqrt(lax.optimization_barrier(jnp.sum(direction * direction, axis=0)) + EPSILON)
        merged = (direction * (magnitude[index] / column_norm)[None, :]).astype(jnp.bfloat16)
        pres.append(project(tokens, merged))
        directions.append(direction)
        norms.append(column_norm)
    gate, up_proj = (pres[0], pres[1])
    sigmoid_g = jax.nn.sigmoid(gate)
    hidden = (gate * sigmoid_g * up_proj).astype(jnp.bfloat16)
    cot_float = hidden_cot.astype(jnp.float32)
    d_pre = [(cot_float * up_proj * sigmoid_g * (1.0 + gate * (1.0 - sigmoid_g))).astype(jnp.bfloat16), (cot_float * gate * sigmoid_g).astype(jnp.bfloat16)]
    grads_in = []
    grads_out = []
    grads_mag = []
    for index in range(2):
        grad_weight = jnp.dot(tokens.T, d_pre[index], preferred_element_type=jnp.float32)
        direction = directions[index]
        column_norm = norms[index]
        statistic = lax.optimization_barrier(jnp.sum(grad_weight * direction, axis=0))
        grads_mag.append(statistic / column_norm)
        coef_grad = magnitude[index] / column_norm
        coef_dir = magnitude[index] * statistic / column_norm ** 3
        d_direction = coef_grad[None, :] * grad_weight - coef_dir[None, :] * direction
        grads_in.append(jnp.dot(adapter_out[index].astype(jnp.float32), d_direction.T, precision=lax.Precision.HIGHEST))
        grads_out.append(jnp.dot(adapter_in[index].astype(jnp.float32), d_direction, precision=lax.Precision.HIGHEST))
    return (hidden, jnp.stack(grads_in), jnp.stack(grads_out), jnp.stack(grads_mag))
```

```python
import functools

import jax
import jax.numpy as jnp
from jax import lax
from jax.experimental import pallas as pl
from jax.experimental.pallas import tpu as pltpu
from jax.sharding import PartitionSpec as P

EPSILON = 1e-06
CHUNKS = 2
VMEM_LIMIT = 48 * 1024 * 1024
BF = jnp.bfloat16
F32 = jnp.float32


def tile_of(width, largest):
    for tile in (1024, 512, 256, 128):
        if tile <= largest and width % tile == 0:
            return tile
    return width


def bit_orders(n):
    bits = [1 << i for i in range(n.bit_length() - 1)]
    return (bits, bits[:1] + bits[1:][::-1])


def block_at(n, order):
    steps = len(order)
    return [sum(order[i] for i in range(steps) if pos >> (steps - 1 - i) & 1) for pos in range(n)]


def swap(x, axis, bit):
    n = lax.axis_size(axis)
    return lax.ppermute(x, axis, [(i, i ^ bit) for i in range(n)])


def dot(a, b, dims=((1,), (0,))):
    return lax.dot_general(a, b, (dims, ((), ())), preferred_element_type=F32)


def split3(x):
    hi = x.astype(BF)
    rest = x - hi.astype(F32)
    mid = rest.astype(BF)
    return hi, mid, (rest - mid.astype(F32)).astype(BF)


def params(**kw):
    return pltpu.CompilerParams(vmem_limit_bytes=VMEM_LIMIT, **kw)


def row_choice(n_blocks, rows, me, order, transpose=False):
    size = n_blocks * rows
    dst = lax.broadcasted_iota(jnp.int32, (size, size), 1 if transpose else 0)
    src = lax.broadcasted_iota(jnp.int32, (size, size), 0 if transpose else 1)
    pos = dst // rows
    block = jnp.zeros_like(pos)
    steps = len(order)
    for i in range(steps):
        block = block + ((pos >> (steps - 1 - i)) & 1) * order[i]
    wanted = (block ^ me) * rows + dst % rows
    return (wanted == src).astype(F32).astype(BF)


def adapter_kernel(n, orders, me_ref, a_ref, w_ref, b_ref, keep_ref, send_ref, sq_ref, aperm, gram):
    rank = a_ref.shape[1]
    half = rank // 2

    @pl.when(pl.program_id(1) == 0)
    def _():
        me = me_ref[0]
        for p in range(2):

            @pl.when(pl.program_id(0) == p)
            def _(p=p):
                choice = row_choice(n, rank // n, me, orders[p])
                aperm[...] = dot(choice, a_ref[0]).astype(BF)

        for i, part in enumerate(split3(dot(aperm[...], a_ref[0], ((1,), (1,))))):
            gram[i] = part

    b = b_ref[0]
    aw = dot(aperm[...], w_ref[0])
    gb = dot(gram[0], b) + dot(gram[1], b) + dot(gram[2], b)
    ad = aw + gb
    keep_ref[0] = ad[:half].astype(BF)
    send_ref[0] = ad[half:].astype(BF)
    both = aw + ad
    squares = jnp.zeros((8, w_ref.shape[2]), F32)
    step = 128
    for i in range(w_ref.shape[1] // step):
        w = w_ref[0, i * step : (i + 1) * step, :].astype(F32)
        squares = squares + jnp.sum((w * w).reshape(step // 8, 8, w.shape[1]), axis=0)
    for p in range(2):

        @pl.when(pl.program_id(0) == p)
        def _(p=p):
            choice = row_choice(n, rank // n, me_ref[0], orders[p])
            cross = both * dot(choice, b)
            sq_ref[0] = jnp.sum(squares, axis=0, keepdims=True) + jnp.sum(cross, axis=0, keepdims=True)


def adapter_call(n, orders, me, a, w, b):
    _, depth, width = w.shape
    rank = a.shape[1]
    tile = tile_of(width, 1024)
    half = jax.ShapeDtypeStruct((2, rank // 2, width), BF)
    return pl.pallas_call(
        functools.partial(adapter_kernel, n, orders),
        grid=(2, width // tile),
        in_specs=[
            pl.BlockSpec(memory_space=pltpu.SMEM),
            pl.BlockSpec((1, rank, depth), lambda p, f: (p, 0, 0)),
            pl.BlockSpec((1, depth, tile), lambda p, f: (p, 0, f)),
            pl.BlockSpec((1, rank, tile), lambda p, f: (p, 0, f)),
        ],
        out_specs=[
            pl.BlockSpec((1, rank // 2, tile), lambda p, f: (p, 0, f)),
            pl.BlockSpec((1, rank // 2, tile), lambda p, f: (p, 0, f)),
            pl.BlockSpec((1, 1, tile), lambda p, f: (p, 0, f)),
        ],
        out_shape=[half, half, jax.ShapeDtypeStruct((2, 1, width), F32)],
        scratch_shapes=[pltpu.VMEM((rank, depth), BF), pltpu.VMEM((3, rank, rank), BF)],
        compiler_params=params(),
        cost_estimate=pl.CostEstimate(
            flops=2 * 4 * rank * depth * width, bytes_accessed=w.size * 2, transcendentals=0
        ),
        name="adapter_pass",
    )(me, a, w, b)


def place_tokens(order, share, me, row, x_refs, x_all):
    steps = len(order)
    per = x_refs[0].shape[0] // share
    for k, x_ref in enumerate(x_refs):
        for h in range(per):
            block = ((row ^ k) * per + h) ^ me
            pos = jnp.int32(0)
            for i in range(steps):
                bit = order[i].bit_length() - 1
                pos = pos + (((block >> bit) & 1) << (steps - 1 - i))
            start = pl.multiple_of(pos * share, share)
            x_all[pl.ds(start, share), :] = x_ref[h * share : (h + 1) * share, :]


def token_kernel(n, share, orders, nx, emit_xa, me_ref, *refs):
    x_refs, (a_ref, w_ref, b_ref) = refs[:nx], refs[nx : nx + 3]
    outs = refs[nx + 3 :]
    keep_ref, send_ref = outs[:2]
    x_all, xa = outs[-2:]
    rank = a_ref.shape[1]
    rows = x_all.shape[0]

    @pl.when(pl.program_id(1) == 0)
    def _():
        me, row = me_ref[0], me_ref[1]
        for p in range(2):

            @pl.when(pl.program_id(0) == p)
            def _(p=p):
                place_tokens(orders[p], share, me, row, x_refs, x_all)

        product = dot(x_all[...], a_ref[0], ((1,), (1,)))
        hi = product.astype(BF)
        xa[0] = hi
        xa[1] = (product - hi.astype(F32)).astype(BF)
        if emit_xa:
            outs[2][0] = product[: rows // 2]
            outs[3][0] = product[rows // 2 :]

    b = b_ref[0]
    y = dot(x_all[...], w_ref[0]) + dot(xa[0], b) + dot(xa[1], b)
    keep_ref[0] = y[: rows // 2].astype(BF)
    send_ref[0] = y[rows // 2 :].astype(BF)


def token_call(n, share, orders, me, xs, a, w, b, first, size, emit_xa):
    _, depth, width = w.shape
    rank = a.shape[1]
    tile = tile_of(size, 512)
    start = first // tile
    rows = n * share
    half = jax.ShapeDtypeStruct((2, rows // 2, size), BF)
    half_spec = pl.BlockSpec((1, rows // 2, tile), lambda p, f: (p, 0, f))
    out_shape, out_specs = [half, half], [half_spec, half_spec]
    if emit_xa:
        out_shape += [jax.ShapeDtypeStruct((2, rows // 2, rank), F32)] * 2
        out_specs += [pl.BlockSpec((1, rows // 2, rank), lambda p, f: (p, 0, 0))] * 2
    return pl.pallas_call(
        functools.partial(token_kernel, n, share, orders, len(xs), emit_xa),
        grid=(2, size // tile),
        in_specs=[pl.BlockSpec(memory_space=pltpu.SMEM)]
        + [pl.BlockSpec(x.shape, lambda p, f: (0, 0)) for x in xs]
        + [
            pl.BlockSpec((1, rank, depth), lambda p, f: (p, 0, 0)),
            pl.BlockSpec((1, depth, tile), lambda p, f: (p, 0, f + start)),
            pl.BlockSpec((1, rank, tile), lambda p, f: (p, 0, f + start)),
        ],
        out_specs=out_specs,
        out_shape=out_shape,
        scratch_shapes=[pltpu.VMEM((rows, depth), BF), pltpu.VMEM((2, rows, rank), BF)],
        compiler_params=params(),
        cost_estimate=pl.CostEstimate(
            flops=4 * rows * depth * size, bytes_accessed=4 * depth * size, transcendentals=0
        ),
        name="token_pass",
    )(me, *xs, a, w, b)


def own_kernel(n, orders, n_parts, has_prior, me_ref, *refs):
    y_refs = refs[: 2 * n_parts]
    xa_ref, sq_ref, mag_ref, b_ref, cot_ref = refs[2 * n_parts : 2 * n_parts + 5]
    outs = refs[2 * n_parts + 5 + has_prior :]
    hid_ref, keep_ref, send_ref, stat_ref, ut_ref, xa = outs
    half = keep_ref.shape[1]
    ys, coefs = [], []
    for p in range(2):
        y = y_refs[p][0].astype(F32)
        for i in range(1, n_parts):
            part = y_refs[2 * i + p]
            y = y + (part[0] if len(part.shape) == 3 else part[...]).astype(F32)
        ys.append(y)
        coefs.append(mag_ref[p] * lax.rsqrt(sq_ref[p] + EPSILON))
    gate, up = ys[0] * coefs[0], ys[1] * coefs[1]
    sig = jax.nn.sigmoid(gate)
    cot = cot_ref[...].astype(F32)
    hid_ref[...] = (gate * sig * up).astype(BF)
    d_pre = (
        (cot * up * sig * (1.0 + gate * (1.0 - sig))).astype(BF),
        (cot * gate * sig).astype(BF),
    )

    @pl.when(pl.program_id(0) == 0)
    def _():
        ut_ref[...] = jnp.zeros_like(ut_ref)
        for p in range(2):
            choice = row_choice(n, xa.shape[2] // n, me_ref[0], orders[p])
            xa[p] = dot(xa_ref[p].astype(BF), choice, ((1,), (1,))).astype(BF)

    for p in range(2):
        d = d_pre[p]
        stat_ref[p] = jnp.sum(d.astype(F32) * ys[p], axis=0, keepdims=True)
        ag = dot(xa[p], d, ((0,), (0,)))
        keep_ref[p] = ag[:half].astype(BF)
        send_ref[p] = ag[half:].astype(BF)
        scaled = (b_ref[p].astype(F32) * coefs[p]).astype(BF)
        ut_ref[p] += dot(d, scaled, ((1,), (1,)))


def own_call(n, orders, me, share, parts, xa, sq, mag, b, cot, prior, first, size):
    width = b.shape[2]
    rank = b.shape[1]
    tile = tile_of(size, 512)
    start = first // tile
    y_args, y_specs = [], []
    for pair in parts:
        for p in range(2):
            part = pair[p]
            y_args.append(part)
            if part.ndim == 3:
                y_specs.append(pl.BlockSpec((1, share, tile), functools.partial(lambda p, f: (p, 0, f), p)))
            else:
                y_specs.append(pl.BlockSpec((share, tile), lambda f: (0, f)))
    half = jax.ShapeDtypeStruct((2, rank // 2, size), BF)
    half_spec = pl.BlockSpec((2, rank // 2, tile), lambda f: (0, 0, f))
    args = [me, *y_args, xa, sq, mag, b, cot]
    specs = [pl.BlockSpec(memory_space=pltpu.SMEM)] + y_specs + [
        pl.BlockSpec(xa.shape, lambda f: (0, 0, 0)),
        pl.BlockSpec((2, 1, tile), lambda f: (0, 0, f + start)),
        pl.BlockSpec((2, 1, tile), lambda f: (0, 0, f + start)),
        pl.BlockSpec((2, rank, tile), lambda f: (0, 0, f + start)),
        pl.BlockSpec((share, tile), lambda f: (0, f + start)),
    ]
    aliases = {}
    if prior is not None:
        aliases = {len(args): 0}
        args.append(prior)
        specs.append(pl.BlockSpec(memory_space=pl.ANY))
    return pl.pallas_call(
        functools.partial(own_kernel, n, orders, len(parts), prior is not None),
        grid=(size // tile,),
        in_specs=specs,
        out_specs=[
            pl.BlockSpec((share, tile), lambda f: (0, f + start)),
            half_spec,
            half_spec,
            pl.BlockSpec((2, 1, tile), lambda f: (0, 0, f)),
            pl.BlockSpec((2, share, rank), lambda f: (0, 0, 0)),
        ],
        out_shape=[
            jax.ShapeDtypeStruct((share, width), BF),
            half,
            half,
            jax.ShapeDtypeStruct((2, 1, size), F32),
            jax.ShapeDtypeStruct((2, share, rank), F32),
        ],
        input_output_aliases=aliases,
        scratch_shapes=[pltpu.VMEM((2, share, rank), BF)],
        compiler_params=params(),
        cost_estimate=pl.CostEstimate(
            flops=4 * rank * share * size * 2, bytes_accessed=share * size * 20, transcendentals=share * size
        ),
        name="own_tokens",
    )(*args)


def second_kernel(w_ref, b_ref, a_ref, cd_ref, out_ref, acc, small):
    last = pl.num_programs(1) - 1

    @pl.when(pl.program_id(1) == 0)
    def _():
        acc[...] = jnp.zeros_like(acc)
        small[...] = jnp.zeros_like(small)

    b = b_ref[0]
    scaled = (b.astype(F32) * cd_ref[0]).astype(BF)
    acc[...] += dot(w_ref[0], scaled, ((1,), (1,)))
    small[...] += dot(b, scaled, ((1,), (1,)))

    @pl.when(pl.program_id(1) == last)
    def _():
        total = acc[...]
        for part in split3(small[...]):
            total = total + dot(a_ref[0], part, ((0,), (0,)))
        out_ref[0] = total


def second_call(w, b, a, cd, first, size):
    _, depth, width = w.shape
    rank = b.shape[1]
    tile = tile_of(size, 512)
    start = first // tile
    return pl.pallas_call(
        second_kernel,
        grid=(2, size // tile),
        in_specs=[
            pl.BlockSpec((1, depth, tile), lambda p, f: (p, 0, f + start)),
            pl.BlockSpec((1, rank, tile), lambda p, f: (p, 0, f + start)),
            pl.BlockSpec((1, rank, depth), lambda p, f: (p, 0, 0)),
            pl.BlockSpec((1, 1, tile), lambda p, f: (p, 0, f)),
        ],
        out_specs=pl.BlockSpec((1, depth, rank), lambda p, f: (p, 0, 0)),
        out_shape=jax.ShapeDtypeStruct((2, depth, rank), F32),
        scratch_shapes=[pltpu.VMEM((depth, rank), F32), pltpu.VMEM((rank, rank), F32)],
        compiler_params=params(),
        cost_estimate=pl.CostEstimate(
            flops=4 * rank * depth * size, bytes_accessed=4 * depth * size, transcendentals=0
        ),
        name="second_pass",
    )(w, b, a, cd)


def join_kernel(share, order, nx, nc, me_ref, *refs):
    x_refs, seconds, ut_refs = refs[:nx], refs[nx : nx + nc], refs[nx + nc : -(nx + 2)]
    outs, (x_all, total) = refs[-(nx + 2) : -2], refs[-2:]
    me, row = me_ref[0], me_ref[1]
    place_tokens(order, share, me, row, x_refs, x_all)
    rank = total.shape[0] // 2
    x = x_all[...]
    for p in range(2):
        ut = jnp.concatenate([ref[p] for ref in ut_refs], axis=0).astype(BF)
        away = seconds[0][p]
        for second in seconds[1:]:
            away = away + second[p]
        total[p * rank : (p + 1) * rank, :] = dot(ut, x, ((0,), (0,))) - away.T
    piece = 2 * rank // nx
    for k in range(nx):
        start = pl.multiple_of((row ^ k) * piece, piece)
        outs[k][...] = total[pl.ds(start, piece), :].astype(outs[k].dtype)


def join_call(share, order, me, xs, seconds, uts):
    depth = xs[0].shape[1]
    rank = seconds[0].shape[2]
    nx = len(xs)
    rows = sum(x.shape[0] for x in xs)
    piece = 2 * rank // nx
    vmem = pl.BlockSpec(memory_space=pltpu.VMEM)
    return pl.pallas_call(
        functools.partial(join_kernel, share, order, nx, len(seconds)),
        in_specs=[pl.BlockSpec(memory_space=pltpu.SMEM)] + [vmem] * (nx + len(seconds) + len(uts)),
        out_specs=[vmem] * nx,
        out_shape=[jax.ShapeDtypeStruct((piece, depth), F32 if k == 0 else BF) for k in range(nx)],
        scratch_shapes=[pltpu.VMEM((rows, depth), BF), pltpu.VMEM((2 * rank, depth), F32)],
        compiler_params=params(),
        name="join_grad_in",
    )(me, *xs, *seconds, *uts)


def lay_kernel(me_ref, *refs):
    out_ref = refs[-1]
    row = me_ref[1]
    for k, ref in enumerate(refs[:-1]):
        piece = ref.shape[0]
        start = pl.multiple_of((row ^ k) * piece, piece)
        out_ref[pl.ds(start, piece), :] = ref[...].astype(F32)


def lay_call(me, pieces):
    rows = sum(x.shape[0] for x in pieces)
    vmem = pl.BlockSpec(memory_space=pltpu.VMEM)
    return pl.pallas_call(
        lay_kernel,
        in_specs=[pl.BlockSpec(memory_space=pltpu.SMEM)] + [vmem] * len(pieces),
        out_specs=vmem,
        out_shape=jax.ShapeDtypeStruct((rows, pieces[0].shape[1]), F32),
        compiler_params=params(),
        name="lay_grad_in",
    )(me, *pieces)


def order_kernel(n, orders, has_prior, me_ref, low_ref, high_ref, *refs):
    out_ref = refs[-1]
    rank = out_ref.shape[1]
    for p in range(2):
        choice = row_choice(n, rank // n, me_ref[0], orders[p], transpose=True)
        both = jnp.concatenate([low_ref[p], high_ref[p]], axis=0)
        out_ref[p] = dot(choice, both)


def order_call(n, orders, me, low, high, prior, first, width):
    _, half, size = low.shape
    tile = tile_of(size, 512)
    start = first // tile
    args = [me, low, high]
    specs = [
        pl.BlockSpec(memory_space=pltpu.SMEM),
        pl.BlockSpec((2, half, tile), lambda f: (0, 0, f)),
        pl.BlockSpec((2, half, tile), lambda f: (0, 0, f)),
    ]
    aliases = {}
    if prior is not None:
        aliases = {3: 0}
        args.append(prior)
        specs.append(pl.BlockSpec(memory_space=pl.ANY))
    return pl.pallas_call(
        functools.partial(order_kernel, n, orders, prior is not None),
        grid=(size // tile,),
        in_specs=specs,
        out_specs=pl.BlockSpec((2, 2 * half, tile), lambda f: (0, 0, f + start)),
        out_shape=jax.ShapeDtypeStruct((2, 2 * half, width), F32),
        input_output_aliases=aliases,
        compiler_params=params(),
        name="order_rows",
    )(*args)


def tied(*xs):
    return lax.optimization_barrier(xs)


def halve(n, orders, keep, send, dtype, extra=()):
    first = swap(send, "col", 1)
    rows = keep.shape[1]
    held = [[keep[p], first[p]] for p in range(2)]
    parts = [(keep, keep), (first, first)]
    for step in range(1, len(orders[0])):
        rows //= 2
        sends = []
        for p in range(2):
            total = sum(part[rows : 2 * rows].astype(F32) for part in held[p])
            sends.append(total.astype(dtype))
        sends = tied(*sends)
        got = tied(*[swap(sends[p], "col", orders[p][step]) for p in range(2)])
        for p in range(2):
            held[p].append(got[p])
        parts.append(tuple(got))
    return parts, rows


def own_rows(parts, rows):
    totals = []
    for p in range(2):
        total = 0.0
        for pair in parts:
            part = pair[p][p] if pair[p].ndim == 3 else pair[p]
            total = total + part[:rows].astype(F32)
        totals.append(total)
    return jnp.stack(totals)


def double_sum(x, bits):
    for bit in bits:
        x = x + swap(x, "col", bit)
    return x


def gather_rows(orders, own):
    held = [own[0], own[1]]
    for step in range(len(orders[0]) - 1, 0, -1):
        sends = tied(*held)
        got = tied(*[swap(sends[p], "col", orders[p][step]) for p in range(2)])
        held = [jnp.concatenate([sends[p], got[p]], axis=0) for p in range(2)]
    low = jnp.stack(held)
    return low, swap(low, "col", 1)


def on_device(tokens, weights, adapter_in, adapter_out, magnitude, hidden_cot):
    n, n_row = lax.axis_size("col"), lax.axis_size("row")
    share = hidden_cot.shape[0]
    width = weights.shape[2]
    orders = bit_orders(n)
    bits = orders[0]
    me = jnp.stack([lax.axis_index("col"), lax.axis_index("row")]).astype(jnp.int32)
    xs = [tokens] + [swap(tokens, "row", k) for k in range(1, n_row)]
    a_keep, a_send, sq_part = adapter_call(n, orders, me, adapter_in, weights, adapter_out)
    squares = double_sum(sq_part, bits)
    a_parts, a_rows = halve(n, orders, a_keep, a_send, BF)
    a_dir = own_rows(a_parts, a_rows)
    mag = magnitude[:, None, :]
    norm = jnp.sqrt(squares + EPSILON)
    coef = mag / norm

    size = width // CHUNKS
    firsts = [c * size for c in range(CHUNKS)]
    y_parts = []
    for c, first in enumerate(firsts):
        outs = token_call(
            n, share, orders, me, xs, adapter_in, weights, adapter_out, first, size, c == 0
        )
        if c == 0:
            xa_parts, _ = halve(n, orders, outs[2], outs[3], F32)
            xa = own_rows(xa_parts, share)
        parts, _ = halve(n, orders, outs[0], outs[1], BF)
        y_parts.append(parts)

    hidden, grad_out, uts, stats, seconds = None, None, [], [], []
    for c, first in enumerate(firsts):
        hidden, g_keep, g_send, stat_part, ut = own_call(
            n, orders, me, share, y_parts[c], xa, squares, mag, adapter_out, hidden_cot, hidden, first, size
        )
        uts.append(ut)
        stat = double_sum(stat_part, bits)
        stats.append(stat)
        span = slice(first, first + size)
        cd = coef[:, :, span] * stat / (norm[:, :, span] ** 2)
        g_parts, g_rows = halve(n, orders, g_keep, g_send, BF)
        own = coef[:, :, span] * own_rows(g_parts, g_rows) - cd * a_dir[:, :, span]
        low, high = gather_rows(orders, own.astype(BF))
        grad_out = order_call(n, orders, me, low, high, grad_out, first, width)
        seconds.append(second_call(weights, adapter_out, adapter_in, cd, first, size))
    grad_mag = (jnp.concatenate(stats, axis=2) / norm)[:, 0, :]

    held = [sum(uts)]
    for bit in bits:
        held = held + [swap(u, "col", bit) for u in held]
    plain = bits[::-1]
    pieces = join_call(share, plain, me, xs, seconds, held)
    total = pieces[0] + sum(swap(pieces[k], "row", k).astype(F32) for k in range(1, n_row))
    total = total.astype(BF)
    laid = lay_call(me, [total] + [swap(total, "row", k) for k in range(1, n_row)])
    grad_in = laid.reshape(2, -1, laid.shape[1])
    return (hidden, grad_in, grad_out, grad_mag)


def solution(mesh):
    in_specs = (
        P("row", "col"),
        P(None, "col", "row"),
        P(None, None, "col"),
        P(None, None, "row"),
        P(None, "row"),
        P("col", "row"),
    )
    out_specs = (P("col", "row"), P(None, None, "col"), P(None, None, "row"), P(None, "row"))
    return jax.shard_map(
        on_device, mesh=mesh, in_specs=in_specs, out_specs=out_specs, check_vma=False
    )
```

```python
import functools
import math

import jax
import jax.numpy as jnp
from jax import lax
from jax.experimental import pallas as pl
from jax.experimental.pallas import tpu as pltpu
from jax.sharding import PartitionSpec as P

EPSILON = 1e-06
QUARTERS = (2, 2)
SLOTS = 4
STEP = 1792
VMEM_LIMIT = 48 * 1024 * 1024
VMEM_FIRST = 62 * 1024 * 1024
BF = jnp.bfloat16
F32 = jnp.float32


def tile_of(width, largest):
    for tile in (1792, 1024, 896, 512, 256, 128):
        if tile <= largest and width % tile == 0:
            return tile
    return width


def bit_orders(n):
    bits = [1 << i for i in range(n.bit_length() - 1)]
    return (bits, bits[:1] + bits[1:][::-1])


def block_at(n, order):
    steps = len(order)
    return [sum(order[i] for i in range(steps) if pos >> (steps - 1 - i) & 1) for pos in range(n)]


def swap(x, axis, bit):
    n = lax.axis_size(axis)
    return lax.ppermute(x, axis, [(i, i ^ bit) for i in range(n)])


def stream(w_ref, buf, sem, step, per, first):
    slots = buf.shape[0]
    ahead = max(slots - 2, 1)
    total = 2 * per
    at = pl.program_id(0) * per + pl.program_id(1)

    def copy(i):
        start = pl.multiple_of(first + (i % per) * step, step)
        return pltpu.make_async_copy(
            w_ref.at[i // per, :, pl.ds(start, step)], buf.at[i % slots], sem.at[i % slots]
        )

    @pl.when(at == 0)
    def _():
        for i in range(min(ahead, total)):
            copy(jnp.int32(i)).start()

    def wait():
        copy(at).wait()

        @pl.when(at + ahead < total)
        def _():
            copy(at + ahead).start()

    return buf.at[at % slots], wait


def stream_scratch(depth, step, total):
    slots = min(SLOTS, total + 1)
    return [pltpu.VMEM((slots, depth, step), BF), pltpu.SemaphoreType.DMA((slots,))]


def dot(a, b, dims=((1,), (0,))):
    return lax.dot_general(a, b, (dims, ((), ())), preferred_element_type=F32)


def split3(x):
    hi = x.astype(BF)
    rest = x - hi.astype(F32)
    mid = rest.astype(BF)
    return hi, mid, (rest - mid.astype(F32)).astype(BF)


def params(limit=VMEM_LIMIT):
    return pltpu.CompilerParams(vmem_limit_bytes=limit)


def row_choice(n_blocks, rows, me, order, transpose=False):
    size = n_blocks * rows
    dst = lax.broadcasted_iota(jnp.int32, (size, size), 1 if transpose else 0)
    src = lax.broadcasted_iota(jnp.int32, (size, size), 0 if transpose else 1)
    pos = dst // rows
    block = jnp.zeros_like(pos)
    steps = len(order)
    for i in range(steps):
        block = block + ((pos >> (steps - 1 - i)) & 1) * order[i]
    wanted = (block ^ me) * rows + dst % rows
    return (wanted == src).astype(F32).astype(BF)


def adapter_kernel(n, orders, step, per, me_ref, a_ref, w_ref, b_ref, ad_ref, sq_ref, aperm, gram, buf, sem):
    rank = a_ref.shape[1]
    w_tile, wait = stream(w_ref, buf, sem, step, per, 0)

    @pl.when(pl.program_id(1) == 0)
    def _():
        for p in range(2):

            @pl.when(pl.program_id(0) == p)
            def _(p=p):
                choice = row_choice(n, rank // n, me_ref[0], orders[p])
                aperm[...] = dot(choice, a_ref[p]).astype(BF)
                for i, part in enumerate(split3(dot(aperm[...], a_ref[p], ((1,), (1,))))):
                    gram[:rank, i * rank : (i + 1) * rank] = part
                gram[rank:, :rank] = choice

        gram[rank:, rank:] = jnp.zeros((rank, 2 * rank), BF)

    wait()
    b = b_ref[0]
    aw = dot(aperm[...], w_tile[...])
    both = dot(gram[...], jnp.concatenate([b, b, b], axis=0))
    ad = aw + both[:rank]
    ad_ref[0] = ad.astype(BF)
    cross = (aw + ad) * both[rank:]
    squares = jnp.zeros((8, step), F32)
    slab = 64
    for i in range(w_tile.shape[0] // slab):
        w = w_tile[i * slab : (i + 1) * slab, :].astype(F32)
        squares = squares + jnp.sum((w * w).reshape(slab // 8, 8, step), axis=0)
    sq_ref[0] = jnp.sum(squares, axis=0, keepdims=True) + jnp.sum(cross, axis=0, keepdims=True)


def adapter_call(n, orders, me, a, w, b):
    _, depth, width = w.shape
    rank = a.shape[1]
    tile = tile_of(width, STEP)
    return pl.pallas_call(
        functools.partial(adapter_kernel, n, orders, tile, width // tile),
        grid=(2, width // tile),
        in_specs=[
            pl.BlockSpec(memory_space=pltpu.SMEM),
            pl.BlockSpec(a.shape, lambda p, f: (0, 0, 0)),
            pl.BlockSpec(memory_space=pl.ANY),
            pl.BlockSpec((1, rank, tile), lambda p, f: (p, 0, f)),
        ],
        out_specs=[
            pl.BlockSpec((1, rank, tile), lambda p, f: (p, 0, f)),
            pl.BlockSpec((1, 1, tile), lambda p, f: (p, 0, f)),
        ],
        out_shape=[
            jax.ShapeDtypeStruct((2, rank, width), BF),
            jax.ShapeDtypeStruct((2, 1, width), F32),
        ],
        scratch_shapes=[pltpu.VMEM((rank, depth), BF), pltpu.VMEM((2 * rank, 3 * rank), BF)]
        + stream_scratch(depth, tile, 2 * (width // tile)),
        compiler_params=params(VMEM_FIRST),
        cost_estimate=pl.CostEstimate(
            flops=2 * 4 * rank * depth * width, bytes_accessed=w.size * 2, transcendentals=0
        ),
        name="adapter_pass",
    )(me, a, w, b)


def place_tokens(order, share, me, row, x_refs, x_all):
    steps = len(order)
    per = x_refs[0].shape[0] // share
    for k, x_ref in enumerate(x_refs):
        for h in range(per):
            block = ((row ^ k) * per + h) ^ me
            pos = jnp.int32(0)
            for i in range(steps):
                bit = order[i].bit_length() - 1
                pos = pos + (((block >> bit) & 1) << (steps - 1 - i))
            start = pl.multiple_of(pos * share, share)
            x_all[pl.ds(start, share), :] = x_ref[h * share : (h + 1) * share, :]


def token_kernel(n, share, orders, nx, emit_xa, step, per, first, me_ref, *refs):
    x_refs, (a_ref, w_ref, b_ref) = refs[:nx], refs[nx : nx + 3]
    outs = refs[nx + 3 :]
    keep_ref, send_ref = outs[:2]
    left, xa, buf, sem = outs[-4:]
    rank = a_ref.shape[1]
    rows = left.shape[0]
    half = rows // 2
    w_tile, wait = stream(w_ref, buf, sem, step, per, first)

    @pl.when(pl.program_id(1) == 0)
    def _():
        me, row = me_ref[0], me_ref[1]
        for p in range(2):

            @pl.when(pl.program_id(0) == p)
            def _(p=p):
                place_tokens(orders[p], share, me, row, x_refs, left)
                if emit_xa and p == 0:
                    both = dot(left[...], a_ref[...].reshape(2 * rank, -1), ((1,), (1,)))
                    outs[2][...] = both[:half]
                    outs[3][...] = both[half:]
                product = dot(left[...], a_ref[p], ((1,), (1,)))
                hi = product.astype(BF)
                xa[:, :rank] = hi
                xa[:, rank:] = (product - hi.astype(F32)).astype(BF)

    wait()
    b = b_ref[0]
    y = dot(left[...], w_tile[...]) + dot(xa[...], jnp.concatenate([b, b], axis=0))
    keep_ref[0] = y[:half].astype(BF)
    send_ref[0] = y[half:].astype(BF)


def token_call(n, share, orders, me, xs, a, w, b, first, size, emit_xa):
    _, depth, width = w.shape
    rank = a.shape[1]
    tile = tile_of(math.gcd(first, size), STEP)
    start = first // tile
    rows = n * share
    half = jax.ShapeDtypeStruct((2, rows // 2, size), BF)
    half_spec = pl.BlockSpec((1, rows // 2, tile), lambda p, f: (p, 0, f))
    out_shape, out_specs = [half, half], [half_spec, half_spec]
    if emit_xa:
        out_shape += [jax.ShapeDtypeStruct((rows // 2, 2 * rank), F32)] * 2
        out_specs += [pl.BlockSpec((rows // 2, 2 * rank), lambda p, f: (0, 0))] * 2
    return pl.pallas_call(
        functools.partial(token_kernel, n, share, orders, len(xs), emit_xa, tile, size // tile, first),
        grid=(2, size // tile),
        in_specs=[pl.BlockSpec(memory_space=pltpu.SMEM)]
        + [pl.BlockSpec(x.shape, lambda p, f: (0, 0)) for x in xs]
        + [
            pl.BlockSpec(a.shape, lambda p, f: (0, 0, 0)),
            pl.BlockSpec(memory_space=pl.ANY),
            pl.BlockSpec((1, rank, tile), lambda p, f: (p, 0, f + start)),
        ],
        out_specs=out_specs,
        out_shape=out_shape,
        scratch_shapes=[pltpu.VMEM((rows, depth), BF), pltpu.VMEM((rows, 2 * rank), BF)]
        + stream_scratch(depth, tile, 2 * (size // tile)),
        compiler_params=params(),
        cost_estimate=pl.CostEstimate(
            flops=4 * rows * depth * size, bytes_accessed=4 * depth * size, transcendentals=0
        ),
        name="token_pass",
    )(me, *xs, a, w, b)


def own_kernel(n, orders, n_parts, n_xa, has_prior, me_ref, *refs):
    y_refs = refs[: 2 * n_parts]
    xa_refs = refs[2 * n_parts : 2 * n_parts + n_xa]
    refs = refs[2 * n_parts + n_xa :]
    sq_ref, mag_ref, b_ref, cot_ref = refs[:4]
    outs = refs[4 + has_prior :]
    hid_ref, keep_ref, send_ref, stat_ref, ut_ref, xa = outs
    half = keep_ref.shape[1]
    ys, coefs = [], []
    for p in range(2):
        y = y_refs[p][0].astype(F32)
        for i in range(1, n_parts):
            part = y_refs[2 * i + p]
            y = y + (part[0] if len(part.shape) == 3 else part[...]).astype(F32)
        ys.append(y)
        coefs.append(mag_ref[p] * lax.rsqrt(sq_ref[p] + EPSILON))
    gate, up = ys[0] * coefs[0], ys[1] * coefs[1]
    sig = jax.nn.sigmoid(gate)
    cot = cot_ref[...].astype(F32)
    hid_ref[...] = (gate * sig * up).astype(BF)
    d_pre = (
        (cot * up * sig * (1.0 + gate * (1.0 - sig))).astype(BF),
        (cot * gate * sig).astype(BF),
    )

    @pl.when(pl.program_id(0) == 0)
    def _():
        ut_ref[...] = jnp.zeros_like(ut_ref)
        rank = xa.shape[2]
        product = xa_refs[0][...]
        for ref in xa_refs[1:]:
            product = product + ref[...]
        product = product.astype(BF)
        for p in range(2):
            choice = row_choice(n, rank // n, me_ref[0], orders[p])
            xa[p] = dot(product[:, p * rank : (p + 1) * rank], choice, ((1,), (1,))).astype(BF)

    for p in range(2):
        d = d_pre[p]
        stat_ref[p] = jnp.sum(d.astype(F32) * ys[p], axis=0, keepdims=True)
        ag = dot(xa[p], d, ((0,), (0,)))
        keep_ref[p] = ag[:half].astype(BF)
        send_ref[p] = ag[half:].astype(BF)
        scaled = (b_ref[p].astype(F32) * coefs[p]).astype(BF)
        ut_ref[p] += dot(d, scaled, ((1,), (1,)))


def own_call(n, orders, me, share, parts, xas, sq, mag, b, cot, prior, first, size):
    width = b.shape[2]
    rank = b.shape[1]
    tile = tile_of(math.gcd(first, size), 1792)
    start = first // tile
    y_args, y_specs = [], []
    for pair in parts:
        for p in range(2):
            part = pair[p]
            y_args.append(part)
            if part.ndim == 3:
                y_specs.append(pl.BlockSpec((1, share, tile), functools.partial(lambda p, f: (p, 0, f), p)))
            else:
                y_specs.append(pl.BlockSpec((share, tile), lambda f: (0, f)))
    half = jax.ShapeDtypeStruct((2, rank // 2, size), BF)
    half_spec = pl.BlockSpec((2, rank // 2, tile), lambda f: (0, 0, f))
    args = [me, *y_args, *xas, sq, mag, b, cot]
    specs = [pl.BlockSpec(memory_space=pltpu.SMEM)] + y_specs
    specs += [pl.BlockSpec((share, x.shape[1]), lambda f: (0, 0)) for x in xas]
    specs += [
        pl.BlockSpec((2, 1, tile), lambda f: (0, 0, f + start)),
        pl.BlockSpec((2, 1, tile), lambda f: (0, 0, f + start)),
        pl.BlockSpec((2, rank, tile), lambda f: (0, 0, f + start)),
        pl.BlockSpec((share, tile), lambda f: (0, f + start)),
    ]
    aliases = {}
    if prior is not None:
        aliases = {len(args): 0}
        args.append(prior)
        specs.append(pl.BlockSpec(memory_space=pl.ANY))
    return pl.pallas_call(
        functools.partial(own_kernel, n, orders, len(parts), len(xas), prior is not None),
        grid=(size // tile,),
        in_specs=specs,
        out_specs=[
            pl.BlockSpec((share, tile), lambda f: (0, f + start)),
            half_spec,
            half_spec,
            pl.BlockSpec((2, 1, tile), lambda f: (0, 0, f)),
            pl.BlockSpec((2, share, rank), lambda f: (0, 0, 0)),
        ],
        out_shape=[
            jax.ShapeDtypeStruct((share, width), BF),
            half,
            half,
            jax.ShapeDtypeStruct((2, 1, size), F32),
            jax.ShapeDtypeStruct((2, share, rank), F32),
        ],
        input_output_aliases=aliases,
        scratch_shapes=[pltpu.VMEM((2, share, rank), BF)],
        compiler_params=params(),
        cost_estimate=pl.CostEstimate(
            flops=4 * rank * share * size * 2, bytes_accessed=share * size * 20, transcendentals=share * size
        ),
        name="own_tokens",
    )(*args)


def second_kernel(step, per, first, token_ref, w_ref, b_ref, a_ref, cd_ref, out_ref, acc, small, buf, sem):
    w_tile, wait = stream(w_ref, buf, sem, step, per, first)
    last = pl.num_programs(1) - 1

    @pl.when(pl.program_id(1) == 0)
    def _():
        acc[...] = jnp.zeros_like(acc)
        small[...] = jnp.zeros_like(small)

    b = b_ref[0]
    scaled = (b.astype(F32) * cd_ref[0]).astype(BF)
    wait()
    acc[...] += dot(scaled, w_tile[...], ((1,), (1,)))
    small[...] += dot(scaled, b, ((1,), (1,)))

    @pl.when(pl.program_id(1) == last)
    def _():
        total = acc[...]
        for part in split3(small[...]):
            total = total + dot(part, a_ref[0])
        out_ref[0] = total


def second_call(w, b, a, cd, first, size, token):
    _, depth, width = w.shape
    rank = b.shape[1]
    tile = tile_of(math.gcd(first, size), STEP)
    start = first // tile
    return pl.pallas_call(
        functools.partial(second_kernel, tile, size // tile, first),
        grid=(2, size // tile),
        in_specs=[
            pl.BlockSpec(memory_space=pltpu.SMEM),
            pl.BlockSpec(memory_space=pl.ANY),
            pl.BlockSpec((1, rank, tile), lambda p, f: (p, 0, f + start)),
            pl.BlockSpec((1, rank, depth), lambda p, f: (p, 0, 0)),
            pl.BlockSpec((1, 1, tile), lambda p, f: (p, 0, f)),
        ],
        out_specs=pl.BlockSpec((1, rank, depth), lambda p, f: (p, 0, 0)),
        out_shape=jax.ShapeDtypeStruct((2, rank, depth), F32),
        scratch_shapes=[pltpu.VMEM((rank, depth), F32), pltpu.VMEM((rank, rank), F32)]
        + stream_scratch(depth, tile, 2 * (size // tile)),
        compiler_params=params(),
        cost_estimate=pl.CostEstimate(
            flops=4 * rank * depth * size, bytes_accessed=4 * depth * size, transcendentals=0
        ),
        name="second_pass",
    )(token, w, b, a, cd)


def join_kernel(share, order, nx, nc, me_ref, *refs):
    x_refs, seconds, ut_refs = refs[:nx], refs[nx : nx + nc], refs[nx + nc : -(nx + 2)]
    outs, (x_all, total) = refs[-(nx + 2) : -2], refs[-2:]
    me, row = me_ref[0], me_ref[1]
    place_tokens(order, share, me, row, x_refs, x_all)
    rank = total.shape[0] // 2
    x = x_all[...]
    for p in range(2):
        ut = ut_refs[0][p].astype(BF)
        away = seconds[0][p]
        for second in seconds[1:]:
            away = away + second[p]
        total[p * rank : (p + 1) * rank, :] = dot(ut, x, ((0,), (0,))) - away
    piece = 2 * rank // nx
    for k in range(nx):
        start = pl.multiple_of((row ^ k) * piece, piece)
        outs[k][...] = total[pl.ds(start, piece), :].astype(outs[k].dtype)


def join_call(share, order, me, xs, seconds, uts):
    depth = xs[0].shape[1]
    rank = seconds[0].shape[1]
    nx = len(xs)
    rows = sum(x.shape[0] for x in xs)
    piece = 2 * rank // nx
    vmem = pl.BlockSpec(memory_space=pltpu.VMEM)
    return pl.pallas_call(
        functools.partial(join_kernel, share, order, nx, len(seconds)),
        in_specs=[pl.BlockSpec(memory_space=pltpu.SMEM)] + [vmem] * (nx + len(seconds) + len(uts)),
        out_specs=[vmem] * nx,
        out_shape=[jax.ShapeDtypeStruct((piece, depth), F32 if k == 0 else BF) for k in range(nx)],
        scratch_shapes=[pltpu.VMEM((rows, depth), BF), pltpu.VMEM((2 * rank, depth), F32)],
        compiler_params=params(),
        name="join_grad_in",
    )(me, *xs, *seconds, *uts)


def lay_kernel(me_ref, *refs):
    out_ref = refs[-1]
    row = me_ref[1]
    for k, ref in enumerate(refs[:-1]):
        piece = ref.shape[0]
        start = pl.multiple_of((row ^ k) * piece, piece)
        out_ref[pl.ds(start, piece), :] = ref[...].astype(F32)


def lay_call(me, pieces):
    rows = sum(x.shape[0] for x in pieces)
    vmem = pl.BlockSpec(memory_space=pltpu.VMEM)
    return pl.pallas_call(
        lay_kernel,
        in_specs=[pl.BlockSpec(memory_space=pltpu.SMEM)] + [vmem] * len(pieces),
        out_specs=vmem,
        out_shape=jax.ShapeDtypeStruct((rows, pieces[0].shape[1]), F32),
        compiler_params=params(),
        name="lay_grad_in",
    )(me, *pieces)


def order_kernel(n, orders, has_prior, me_ref, low_ref, high_ref, *refs):
    out_ref = refs[-1]
    rank = out_ref.shape[1]
    for p in range(2):
        choice = row_choice(n, rank // n, me_ref[0], orders[p], transpose=True)
        both = jnp.concatenate([low_ref[p], high_ref[p]], axis=0)
        out_ref[p] = dot(choice, both)


def order_call(n, orders, me, low, high, prior, first, width):
    _, half, size = low.shape
    tile = tile_of(math.gcd(first, size), 1792)
    start = first // tile
    args = [me, low, high]
    specs = [
        pl.BlockSpec(memory_space=pltpu.SMEM),
        pl.BlockSpec((2, half, tile), lambda f: (0, 0, f)),
        pl.BlockSpec((2, half, tile), lambda f: (0, 0, f)),
    ]
    aliases = {}
    if prior is not None:
        aliases = {3: 0}
        args.append(prior)
        specs.append(pl.BlockSpec(memory_space=pl.ANY))
    return pl.pallas_call(
        functools.partial(order_kernel, n, orders, prior is not None),
        grid=(size // tile,),
        in_specs=specs,
        out_specs=pl.BlockSpec((2, 2 * half, tile), lambda f: (0, 0, f + start)),
        out_shape=jax.ShapeDtypeStruct((2, 2 * half, width), F32),
        input_output_aliases=aliases,
        compiler_params=params(),
        name="order_rows",
    )(*args)


def tied(*xs):
    return lax.optimization_barrier(xs)


class Turn:
    def __init__(self, token):
        self.token = token

    def pass_on(self, *xs):
        self.token, *xs = tied(self.token, *xs)
        return tuple(xs)


class Halving:
    def __init__(self, orders, keep, send, dtype=BF):
        self.flat = keep.ndim == 2
        self.orders, self.dtype = orders[:1] if self.flat else orders, dtype
        self.parts = [(keep,) if self.flat else (keep[0], keep[1])]
        self.whole = [keep]
        self.send, self.step, self.rows = [send], 0, keep.shape[0 if self.flat else 1]

    def sums(self, low, high):
        return [sum(part[p][low:high].astype(F32) for part in self.parts) for p in range(len(self.orders))]

    def prepare(self):
        if self.step:
            self.rows //= 2
            self.send = [x.astype(self.dtype) for x in self.sums(self.rows, 2 * self.rows)]
        return self.send

    def go(self, send):
        if self.step:
            self.got = [swap(x, "col", order[self.step]) for x, order in zip(send, self.orders)]
        else:
            self.got = [swap(send[0], "col", self.orders[0][0])]
        return self.got

    def arrived(self, got):
        if self.step or self.flat:
            self.parts.append(tuple(got))
            self.whole.append(tuple(got) if len(got) > 1 else got[0])
        else:
            self.parts.append((got[0][0], got[0][1]))
            self.whole.append(got[0])
        self.step += 1

    def done(self):
        return self.step == len(self.orders[0])

    def own(self):
        return self.sums(0, self.rows)

    def pairs(self):
        return [x if isinstance(x, tuple) else (x, x) for x in self.whole]


class Doubling:
    def __init__(self, bits, x, direct=False):
        self.bits, self.x, self.step = [[bit] for bit in bits], x, 0
        if direct:
            self.bits = [bits[:1], list(range(2, 1 << len(bits), 2))]

    def prepare(self):
        return [self.x]

    def go(self, send):
        self.x = send[0]
        return [swap(send[0], "col", bit) for bit in self.bits[self.step]]

    def arrived(self, got):
        self.x = self.x + sum(got)
        self.step += 1

    def done(self):
        return self.step == len(self.bits)


class Scattering:
    def __init__(self, orders, n, keep, send):
        self.orders, self.keep, self.step = orders, keep, 0
        self.send, self.n = send, n

    def prepare(self):
        if self.step == 0:
            return [self.send]
        self.sum = self.keep.astype(F32) + self.first.astype(F32)
        rows = self.sum.shape[1] * 2 // self.n
        out = []
        for j in range(2, self.n, 2):
            at = [block_at(self.n, order).index(j) * rows for order in self.orders]
            both = [self.sum[p, at[p] : at[p] + rows] for p in range(2)]
            out.append(jnp.concatenate(both, axis=0).astype(BF))
        self.rows = rows
        return out

    def go(self, send):
        if self.step == 0:
            return [swap(send[0], "col", 1)]
        return [swap(x, "col", j) for x, j in zip(send, range(2, self.n, 2))]

    def arrived(self, got):
        if self.step == 0:
            self.first = got[0]
        else:
            rows = self.rows
            total = sum(x.astype(F32) for x in got)
            self.own = [(self.sum[p, :rows] + total[p * rows : (p + 1) * rows]).astype(BF) for p in range(2)]
        self.step += 1

    def done(self):
        return self.step == 2


class Collecting:
    def __init__(self, bits, x):
        self.bits, self.x, self.step = bits, x, 0

    def prepare(self):
        return [self.x]

    def go(self, send):
        self.x = send[0]
        return [swap(send[0], "col", self.bits[self.step])]

    def arrived(self, got):
        self.x = jnp.concatenate([self.x, got[0]], axis=1)
        self.step += 1

    def done(self):
        return self.step == len(self.bits)


class Laying:
    def __init__(self, orders, own):
        self.orders, self.held, self.step = orders, own, len(orders[0]) - 1

    def prepare(self):
        return self.held if self.step else [jnp.stack(self.held)]

    def go(self, send):
        self.held = list(send)
        if self.step:
            return [swap(x, "col", order[self.step]) for x, order in zip(send, self.orders)]
        return [swap(send[0], "col", self.orders[0][0])]

    def arrived(self, got):
        if self.step:
            self.held = [jnp.concatenate(pair, axis=0) for pair in zip(self.held, got)]
        else:
            self.held += list(got)
        self.step -= 1

    def done(self):
        return self.step < 0


class Around:
    def __init__(self, n, xs):
        self.n, self.xs, self.got = n, xs, None

    def prepare(self):
        return self.xs

    def go(self, send):
        return [swap(x, "row", k) for k, x in enumerate(send, start=1)]

    def arrived(self, got):
        self.got = list(got)

    def done(self):
        return self.got is not None


def phase(turn, moves, kernel=None):
    moves = [move for move in moves if not move.done()]
    sends = [move.prepare() for move in moves]
    sent = list(turn.pass_on(*[x for send in sends for x in send]))
    got = [move.go([sent.pop(0) for _ in send]) for move, send in zip(moves, sends)]
    outs = kernel(turn.token) if kernel else ()
    flat = list(turn.pass_on(*[x for g in got for x in g], *outs))
    for move, g in zip(moves, got):
        move.arrived([flat.pop(0) for _ in g])
    return flat


def on_device(tokens, weights, adapter_in, adapter_out, magnitude, hidden_cot):
    n, n_row = lax.axis_size("col"), lax.axis_size("row")
    rank = adapter_in.shape[1]
    share = hidden_cot.shape[0]
    width = weights.shape[2]
    orders = bit_orders(n)
    bits = orders[0]
    steps = len(bits)
    me = jnp.stack([lax.axis_index("col"), lax.axis_index("row")]).astype(jnp.int32)
    mag = magnitude[:, None, :]
    sizes = [width * q // sum(QUARTERS) for q in QUARTERS]
    firsts = [sum(sizes[:c]) for c in range(len(sizes))]
    count = len(sizes)

    xs = [tokens] + [swap(tokens, "row", k) for k in range(1, n_row)]
    ad, sq = adapter_call(n, orders, me, adapter_in, weights, adapter_out)
    turn = Turn(me)
    *xs, sq = turn.pass_on(*xs, sq)
    squares = Doubling(bits, sq)

    def project(c):
        return lambda token: token_call(
            n, share, orders, token, xs, adapter_in, weights, adapter_out, firsts[c], sizes[c], c == 0
        )

    def elementwise(c):
        return lambda token: own_call(
            n, orders, token, share, halvings[c].pairs(), [x[0] for x in xa.parts], squares.x, mag, adapter_out,
            hidden_cot, hidden, firsts[c], sizes[c],
        )

    def second(c):
        first, size = firsts[c], sizes[c]
        return lambda token: [
            second_call(weights, adapter_out, adapter_in, cd[:, :, first : first + size], first, size, token)
        ]

    outs = phase(turn, [squares], project(0))
    halvings = [Halving(orders, outs[0], outs[1])]
    xa = Halving(orders, outs[2], outs[3], F32)
    moves = [squares, xa, halvings[0]]
    phase(turn, moves)
    for c in range(1, count):
        outs = phase(turn, moves, project(c))
        halvings.append(Halving(orders, outs[0], outs[1]))
        moves.append(halvings[-1])
        phase(turn, moves)
    hidden, results = None, []
    for c in range(count):
        while not (halvings[c].done() and squares.done() and xa.done()):
            phase(turn, moves)
        hidden, *outs = phase(turn, moves, elementwise(c))
        results.append(outs)
    stats = Doubling(bits, jnp.concatenate([r[2] for r in results], axis=2), direct=True)
    uts = Collecting(bits, sum(r[3] for r in results))
    while not stats.done():
        phase(turn, [stats, uts])

    norm = jnp.sqrt(squares.x + EPSILON)
    coef = mag / norm
    cd = coef * stats.x / (norm * norm)
    half = rank // 2
    folded = []
    for i in range(2):
        g = jnp.concatenate([r[i] for r in results], axis=2).astype(F32)
        folded.append((coef * g - cd * ad[:, i * half : (i + 1) * half].astype(F32)).astype(BF))
    turning = Scattering(orders, n, *folded)
    while not uts.done():
        phase(turn, [turning, uts])
    seconds = phase(
        turn,
        [turning],
        lambda token: [second_call(weights, adapter_out, adapter_in, cd, 0, width, token)],
    )
    laying = Laying(orders, turning.own)
    pieces = turn.pass_on(*join_call(share, bits[::-1], turn.token, xs, seconds, [uts.x]))
    away = Around(n_row, pieces[1:])
    phase(turn, [laying, away])
    total = (pieces[0] + sum(x.astype(F32) for x in away.got)).astype(BF)
    back = Around(n_row, [total] * (n_row - 1))
    while laying.step or not back.done():
        phase(turn, [laying, back])
    (grad_in,) = phase(turn, [laying], lambda token: [lay_call(token, [total] + back.got)])
    grad_in = grad_in.reshape(2, -1, grad_in.shape[1])
    low, high = laying.held
    grad_out = order_call(n, orders, me, low, high, None, 0, width)
    grad_mag = (stats.x / norm)[:, 0, :]
    return (hidden, grad_in, grad_out, grad_mag)


def solution(mesh):
    in_specs = (
        P("row", "col"),
        P(None, "col", "row"),
        P(None, None, "col"),
        P(None, None, "row"),
        P(None, "row"),
        P("col", "row"),
    )
    out_specs = (P("col", "row"), P(None, None, "col"), P(None, None, "row"), P(None, "row"))
    return jax.shard_map(
        on_device, mesh=mesh, in_specs=in_specs, out_specs=out_specs, check_vma=False
    )
```

```python
import functools
import math

import jax
import jax.numpy as jnp
from jax import lax
from jax.experimental import pallas as pl
from jax.experimental.pallas import tpu as pltpu
from jax.sharding import PartitionSpec as P

EPSILON = 1e-06
QUARTERS = (2, 2)
SLOTS = 4
STEP = 1792
VMEM_LIMIT = 48 * 1024 * 1024
VMEM_FIRST = 62 * 1024 * 1024
BF = jnp.bfloat16
F32 = jnp.float32


def tile_of(width, largest):
    for tile in (3584, 1792, 1024, 896, 512, 256, 128):
        if tile <= largest and width % tile == 0:
            return tile
    return width


def bit_orders(n):
    bits = [1 << i for i in range(n.bit_length() - 1)]
    return (bits, bits[:1] + bits[1:][::-1])


def block_at(n, order):
    steps = len(order)
    return [sum(order[i] for i in range(steps) if pos >> (steps - 1 - i) & 1) for pos in range(n)]


def swap(x, axis, bit):
    n = lax.axis_size(axis)
    return lax.ppermute(x, axis, [(i, i ^ bit) for i in range(n)])


def stream(w_ref, buf, sem, step, per, first):
    slots = buf.shape[0]
    ahead = max(slots - 2, 1)
    total = 2 * per
    at = pl.program_id(0) * per + pl.program_id(1)

    def copy(i):
        start = pl.multiple_of(first + (i % per) * step, step)
        return pltpu.make_async_copy(
            w_ref.at[i // per, :, pl.ds(start, step)], buf.at[i % slots], sem.at[i % slots]
        )

    @pl.when(at == 0)
    def _():
        for i in range(min(ahead, total)):
            copy(jnp.int32(i)).start()

    def wait():
        copy(at).wait()

        @pl.when(at + ahead < total)
        def _():
            copy(at + ahead).start()

    return buf.at[at % slots], wait


class Stream:
    def __init__(self, w_ref, buf, sem, step, per, first):
        self.w_ref, self.buf, self.sem = w_ref, buf, sem
        self.step, self.per, self.first = step, per, first
        self.slots, self.total = buf.shape[0], 2 * per
        self.ahead = max(self.slots - 2, 1)
        for i in range(min(self.ahead, self.total)):
            self.copy(jnp.int32(i)).start()

    def copy(self, i):
        start = pl.multiple_of(self.first + (i % self.per) * self.step, self.step)
        slot = i % self.slots
        return pltpu.make_async_copy(
            self.w_ref.at[i // self.per, :, pl.ds(start, self.step)], self.buf.at[slot], self.sem.at[slot]
        )

    def over(self, p, body):
        @pl.loop(0, self.per)
        def _(f):
            at = p * self.per + f
            self.copy(at).wait()

            @pl.when(at + self.ahead < self.total)
            def _():
                self.copy(at + self.ahead).start()

            start = pl.multiple_of(f * self.step, self.step)
            whole = pl.ds(pl.multiple_of(self.first + start, self.step), self.step)
            body(self.buf.at[at % self.slots], whole, pl.ds(start, self.step))


def stream_scratch(depth, step, total):
    slots = min(SLOTS, total + 1)
    return [pltpu.VMEM((slots, depth, step), BF), pltpu.SemaphoreType.DMA((slots,))]


def dot(a, b, dims=((1,), (0,))):
    return lax.dot_general(a, b, (dims, ((), ())), preferred_element_type=F32)


def split3(x):
    hi = x.astype(BF)
    rest = x - hi.astype(F32)
    mid = rest.astype(BF)
    return hi, mid, (rest - mid.astype(F32)).astype(BF)


def params(limit=VMEM_LIMIT):
    return pltpu.CompilerParams(vmem_limit_bytes=limit)


def row_choice(n_blocks, rows, me, order, transpose=False):
    size = n_blocks * rows
    dst = lax.broadcasted_iota(jnp.int32, (size, size), 1 if transpose else 0)
    src = lax.broadcasted_iota(jnp.int32, (size, size), 0 if transpose else 1)
    pos = dst // rows
    block = jnp.zeros_like(pos)
    steps = len(order)
    for i in range(steps):
        block = block + ((pos >> (steps - 1 - i)) & 1) * order[i]
    wanted = (block ^ me) * rows + dst % rows
    return (wanted == src).astype(F32).astype(BF)


def adapter_kernel(n, orders, step, per, me_ref, a_ref, w_ref, b_ref, keep_ref, send_ref, sq_ref, aperm, gram, buf, sem):
    rank = a_ref.shape[1]
    w_tile, wait = stream(w_ref, buf, sem, step, per, 0)

    @pl.when(pl.program_id(1) == 0)
    def _():
        for p in range(2):

            @pl.when(pl.program_id(0) == p)
            def _(p=p):
                choice = row_choice(n, rank // n, me_ref[0], orders[p])
                aperm[...] = dot(choice, a_ref[p]).astype(BF)
                for i, part in enumerate(split3(dot(aperm[...], a_ref[p], ((1,), (1,))))):
                    gram[:rank, i * rank : (i + 1) * rank] = part
                gram[rank:, :rank] = choice

        gram[rank:, rank:] = jnp.zeros((rank, 2 * rank), BF)

    wait()
    b = b_ref[0]
    aw = dot(aperm[...], w_tile[...])
    squares = jnp.zeros((8, step), F32)
    slab = 64
    for i in range(w_tile.shape[0] // slab):
        w = w_tile[i * slab : (i + 1) * slab, :].astype(F32)
        squares = squares + jnp.sum((w * w).reshape(slab // 8, 8, step), axis=0)
    both = dot(gram[...], jnp.concatenate([b, b, b], axis=0))
    ad = aw + both[:rank]
    keep_ref[0] = ad[: rank // 2].astype(BF)
    send_ref[0] = ad[rank // 2 :].astype(BF)
    cross = (aw + ad) * both[rank:]
    sq_ref[0] = jnp.sum(squares, axis=0, keepdims=True) + jnp.sum(cross, axis=0, keepdims=True)


def adapter_call(n, orders, me, a, w, b):
    _, depth, width = w.shape
    rank = a.shape[1]
    tile = tile_of(width, STEP)
    return pl.pallas_call(
        functools.partial(adapter_kernel, n, orders, tile, width // tile),
        grid=(2, width // tile),
        in_specs=[
            pl.BlockSpec(memory_space=pltpu.SMEM),
            pl.BlockSpec(a.shape, lambda p, f: (0, 0, 0)),
            pl.BlockSpec(memory_space=pl.ANY),
            pl.BlockSpec((1, rank, tile), lambda p, f: (p, 0, f)),
        ],
        out_specs=[
            pl.BlockSpec((1, rank // 2, tile), lambda p, f: (p, 0, f)),
            pl.BlockSpec((1, rank // 2, tile), lambda p, f: (p, 0, f)),
            pl.BlockSpec((1, 1, tile), lambda p, f: (p, 0, f)),
        ],
        out_shape=[
            jax.ShapeDtypeStruct((2, rank // 2, width), BF),
            jax.ShapeDtypeStruct((2, rank // 2, width), BF),
            jax.ShapeDtypeStruct((2, 1, width), F32),
        ],
        scratch_shapes=[pltpu.VMEM((rank, depth), BF), pltpu.VMEM((2 * rank, 3 * rank), BF)]
        + stream_scratch(depth, tile, 2 * (width // tile)),
        compiler_params=params(VMEM_FIRST),
        cost_estimate=pl.CostEstimate(
            flops=2 * 4 * rank * depth * width, bytes_accessed=w.size * 2, transcendentals=0
        ),
        name="adapter_pass",
    )(me, a, w, b)


def place_tokens(order, share, me, row, x_refs, x_all):
    steps = len(order)
    per = x_refs[0].shape[0] // share
    for k, x_ref in enumerate(x_refs):
        for h in range(per):
            block = ((row ^ k) * per + h) ^ me
            pos = jnp.int32(0)
            for i in range(steps):
                bit = order[i].bit_length() - 1
                pos = pos + (((block >> bit) & 1) << (steps - 1 - i))
            start = pl.multiple_of(pos * share, share)
            x_all[pl.ds(start, share), :] = x_ref[h * share : (h + 1) * share, :]


def token_kernel(n, share, orders, nx, emit_xa, step, per, first, me_ref, *refs):
    x_refs, (a_ref, w_ref, b_ref) = refs[:nx], refs[nx : nx + 3]
    outs = refs[nx + 3 :]
    keep_ref, send_ref = outs[:2]
    left, xa, buf, sem = outs[-4:]
    rank = a_ref.shape[1]
    rows = left.shape[0]
    half = rows // 2
    w_tile, wait = stream(w_ref, buf, sem, step, per, first)

    @pl.when(pl.program_id(1) == 0)
    def _():
        me, row = me_ref[0], me_ref[1]
        for p in range(2):

            @pl.when(pl.program_id(0) == p)
            def _(p=p):
                place_tokens(orders[p], share, me, row, x_refs, left)
                if emit_xa and p == 0:
                    both = dot(left[...], a_ref[...].reshape(2 * rank, -1), ((1,), (1,)))
                    outs[2][...] = both[:half]
                    outs[3][...] = both[half:]
                product = dot(left[...], a_ref[p], ((1,), (1,)))
                hi = product.astype(BF)
                xa[:, :rank] = hi
                xa[:, rank:] = (product - hi.astype(F32)).astype(BF)

    wait()
    b = b_ref[0]
    y = dot(left[...], w_tile[...]) + dot(xa[...], jnp.concatenate([b, b], axis=0))
    keep_ref[0] = y[:half].astype(BF)
    send_ref[0] = y[half:].astype(BF)


def token_call(n, share, orders, me, xs, a, w, b, first, size, emit_xa):
    _, depth, width = w.shape
    rank = a.shape[1]
    tile = tile_of(math.gcd(first, size), STEP)
    start = first // tile
    rows = n * share
    half = jax.ShapeDtypeStruct((2, rows // 2, size), BF)
    half_spec = pl.BlockSpec((1, rows // 2, tile), lambda p, f: (p, 0, f))
    out_shape, out_specs = [half, half], [half_spec, half_spec]
    if emit_xa:
        out_shape += [jax.ShapeDtypeStruct((rows // 2, 2 * rank), F32)] * 2
        out_specs += [pl.BlockSpec((rows // 2, 2 * rank), lambda p, f: (0, 0))] * 2
    return pl.pallas_call(
        functools.partial(token_kernel, n, share, orders, len(xs), emit_xa, tile, size // tile, first),
        grid=(2, size // tile),
        in_specs=[pl.BlockSpec(memory_space=pltpu.SMEM)]
        + [pl.BlockSpec(x.shape, lambda p, f: (0, 0)) for x in xs]
        + [
            pl.BlockSpec(a.shape, lambda p, f: (0, 0, 0)),
            pl.BlockSpec(memory_space=pl.ANY),
            pl.BlockSpec((1, rank, tile), lambda p, f: (p, 0, f + start)),
        ],
        out_specs=out_specs,
        out_shape=out_shape,
        scratch_shapes=[pltpu.VMEM((rows, depth), BF), pltpu.VMEM((rows, 2 * rank), BF)]
        + stream_scratch(depth, tile, 2 * (size // tile)),
        compiler_params=params(),
        cost_estimate=pl.CostEstimate(
            flops=4 * rows * depth * size, bytes_accessed=4 * depth * size, transcendentals=0
        ),
        name="token_pass",
    )(me, *xs, a, w, b)


def own_kernel(n, orders, n_parts, n_xa, has_prior, me_ref, *refs):
    y_refs = refs[: 2 * n_parts]
    xa_refs = refs[2 * n_parts : 2 * n_parts + n_xa]
    refs = refs[2 * n_parts + n_xa :]
    sq_ref, mag_ref, b_ref, cot_ref = refs[:4]
    outs = refs[4 + has_prior :]
    hid_ref, keep_ref, send_ref, stat_ref, ut_ref, xa = outs
    half = keep_ref.shape[1]
    ys, coefs = [], []
    for p in range(2):
        y = y_refs[p][0].astype(F32)
        for i in range(1, n_parts):
            part = y_refs[2 * i + p]
            y = y + (part[0] if len(part.shape) == 3 else part[...]).astype(F32)
        ys.append(y)
        coefs.append(mag_ref[p] * lax.rsqrt(sq_ref[p] + EPSILON))
    gate, up = ys[0] * coefs[0], ys[1] * coefs[1]
    sig = jax.nn.sigmoid(gate)
    cot = cot_ref[...].astype(F32)
    hid_ref[...] = (gate * sig * up).astype(BF)
    d_pre = (
        (cot * up * sig * (1.0 + gate * (1.0 - sig))).astype(BF),
        (cot * gate * sig).astype(BF),
    )

    @pl.when(pl.program_id(0) == 0)
    def _():
        ut_ref[...] = jnp.zeros_like(ut_ref)
        rank = xa.shape[2]
        product = xa_refs[0][...]
        for ref in xa_refs[1:]:
            product = product + ref[...]
        product = product.astype(BF)
        for p in range(2):
            choice = row_choice(n, rank // n, me_ref[0], orders[p])
            xa[p] = dot(product[:, p * rank : (p + 1) * rank], choice, ((1,), (1,))).astype(BF)

    for p in range(2):
        d = d_pre[p]
        stat_ref[p] = jnp.sum(d.astype(F32) * ys[p], axis=0, keepdims=True)
        ag = dot(xa[p], d, ((0,), (0,)))
        keep_ref[p] = ag[:half].astype(BF)
        send_ref[p] = ag[half:].astype(BF)
        scaled = (b_ref[p].astype(F32) * coefs[p]).astype(BF)
        rank = scaled.shape[0]
        ut_ref[:, p * rank : (p + 1) * rank] += dot(d, scaled, ((1,), (1,)))


def own_call(n, orders, me, share, parts, xas, sq, mag, b, cot, prior, first, size):
    width = b.shape[2]
    rank = b.shape[1]
    tile = tile_of(math.gcd(first, size), 3584)
    start = first // tile
    y_args, y_specs = [], []
    for pair in parts:
        for p in range(2):
            part = pair[p]
            y_args.append(part)
            if part.ndim == 3:
                y_specs.append(pl.BlockSpec((1, share, tile), functools.partial(lambda p, f: (p, 0, f), p)))
            else:
                y_specs.append(pl.BlockSpec((share, tile), lambda f: (0, f)))
    half = jax.ShapeDtypeStruct((2, rank // 2, size), BF)
    half_spec = pl.BlockSpec((2, rank // 2, tile), lambda f: (0, 0, f))
    args = [me, *y_args, *xas, sq, mag, b, cot]
    specs = [pl.BlockSpec(memory_space=pltpu.SMEM)] + y_specs
    specs += [pl.BlockSpec((share, x.shape[1]), lambda f: (0, 0)) for x in xas]
    specs += [
        pl.BlockSpec((2, 1, tile), lambda f: (0, 0, f + start)),
        pl.BlockSpec((2, 1, tile), lambda f: (0, 0, f + start)),
        pl.BlockSpec((2, rank, tile), lambda f: (0, 0, f + start)),
        pl.BlockSpec((share, tile), lambda f: (0, f + start)),
    ]
    aliases = {}
    if prior is not None:
        aliases = {len(args): 0}
        args.append(prior)
        specs.append(pl.BlockSpec(memory_space=pl.ANY))
    return pl.pallas_call(
        functools.partial(own_kernel, n, orders, len(parts), len(xas), prior is not None),
        grid=(size // tile,),
        in_specs=specs,
        out_specs=[
            pl.BlockSpec((share, tile), lambda f: (0, f + start)),
            half_spec,
            half_spec,
            pl.BlockSpec((2, 1, tile), lambda f: (0, 0, f)),
            pl.BlockSpec((share, 2 * rank), lambda f: (0, 0)),
        ],
        out_shape=[
            jax.ShapeDtypeStruct((share, width), BF),
            half,
            half,
            jax.ShapeDtypeStruct((2, 1, size), F32),
            jax.ShapeDtypeStruct((share, 2 * rank), F32),
        ],
        input_output_aliases=aliases,
        scratch_shapes=[pltpu.VMEM((2, share, rank), BF)],
        compiler_params=params(),
        cost_estimate=pl.CostEstimate(
            flops=4 * rank * share * size * 2, bytes_accessed=share * size * 20, transcendentals=share * size
        ),
        name="own_tokens",
    )(*args)


def second_kernel(step, per, first, token_ref, w_ref, b_ref, a_ref, cd_ref, out_ref, small, buf, sem):
    tiles = Stream(w_ref, buf, sem, step, per, first)
    for p in range(2):
        out_ref[p] = jnp.zeros(out_ref.shape[1:], F32)
        small[...] = jnp.zeros_like(small)

        def body(w_tile, whole, _, p=p):
            b = b_ref[p, :, whole]
            scaled = (b.astype(F32) * cd_ref[p, :, whole]).astype(BF)
            out_ref[p] += dot(scaled, w_tile[...], ((1,), (1,)))
            small[...] += dot(scaled, b, ((1,), (1,)))

        tiles.over(p, body)
        parts = jnp.concatenate(split3(small[...]), axis=1)
        out_ref[p] += dot(parts, jnp.concatenate([a_ref[p]] * 3, axis=0))


def second_call(w, b, a, cd, first, size, token):
    _, depth, width = w.shape
    rank = b.shape[1]
    tile = tile_of(math.gcd(first, size), STEP)
    vmem = pl.BlockSpec(memory_space=pltpu.VMEM)
    return pl.pallas_call(
        functools.partial(second_kernel, tile, size // tile, first),
        in_specs=[pl.BlockSpec(memory_space=pltpu.SMEM), pl.BlockSpec(memory_space=pl.ANY), vmem, vmem, vmem],
        out_specs=vmem,
        out_shape=jax.ShapeDtypeStruct((2, rank, depth), F32),
        scratch_shapes=[pltpu.VMEM((rank, rank), F32)] + stream_scratch(depth, tile, 2 * (size // tile)),
        compiler_params=params(),
        cost_estimate=pl.CostEstimate(
            flops=4 * rank * depth * size, bytes_accessed=4 * depth * size, transcendentals=0
        ),
        name="second_pass",
    )(token, w, b, a, cd)


def join_kernel(share, order, nx, nc, me_ref, *refs):
    x_refs, seconds, ut_refs = refs[:nx], refs[nx : nx + nc], refs[nx + nc : -(nx + 2)]
    outs, (x_all, total) = refs[-(nx + 2) : -2], refs[-2:]
    me, row = me_ref[0], me_ref[1]
    place_tokens(order, share, me, row, x_refs, x_all)
    rank = total.shape[0] // 2
    x = x_all[...]
    for p in range(2):
        ut = ut_refs[0][:, p * rank : (p + 1) * rank].astype(BF)
        away = seconds[0][p]
        for second in seconds[1:]:
            away = away + second[p]
        total[p * rank : (p + 1) * rank, :] = dot(ut, x, ((0,), (0,))) - away
    piece = 2 * rank // nx
    for k in range(nx):
        start = pl.multiple_of((row ^ k) * piece, piece)
        outs[k][...] = total[pl.ds(start, piece), :].astype(outs[k].dtype)


def join_call(share, order, me, xs, seconds, uts):
    depth = xs[0].shape[1]
    rank = seconds[0].shape[1]
    nx = len(xs)
    rows = sum(x.shape[0] for x in xs)
    piece = 2 * rank // nx
    vmem = pl.BlockSpec(memory_space=pltpu.VMEM)
    return pl.pallas_call(
        functools.partial(join_kernel, share, order, nx, len(seconds)),
        in_specs=[pl.BlockSpec(memory_space=pltpu.SMEM)] + [vmem] * (nx + len(seconds) + len(uts)),
        out_specs=[vmem] * nx,
        out_shape=[jax.ShapeDtypeStruct((piece, depth), F32 if k == 0 else BF) for k in range(nx)],
        scratch_shapes=[pltpu.VMEM((rows, depth), BF), pltpu.VMEM((2 * rank, depth), F32)],
        compiler_params=params(),
        name="join_grad_in",
    )(me, *xs, *seconds, *uts)


def lay_kernel(me_ref, *refs):
    out_ref = refs[-1]
    row = me_ref[1]
    for k, ref in enumerate(refs[:-1]):
        piece = ref.shape[0]
        start = pl.multiple_of((row ^ k) * piece, piece)
        out_ref[pl.ds(start, piece), :] = ref[...].astype(F32)


def lay_call(me, pieces):
    rows = sum(x.shape[0] for x in pieces)
    vmem = pl.BlockSpec(memory_space=pltpu.VMEM)
    return pl.pallas_call(
        lay_kernel,
        in_specs=[pl.BlockSpec(memory_space=pltpu.SMEM)] + [vmem] * len(pieces),
        out_specs=vmem,
        out_shape=jax.ShapeDtypeStruct((rows, pieces[0].shape[1]), F32),
        compiler_params=params(),
        name="lay_grad_in",
    )(me, *pieces)


def fold_kernel(n, orders, *refs):
    (ad_keep, ad_got, g_keep, g_got, sq_ref, stat_ref, mag_ref), outs = refs[:7], refs[7:]
    cd_ref, blocks = outs[0], outs[1:]
    rows = g_keep.shape[1] * 2 // n
    totals = []
    for p in range(2):
        inverse = lax.rsqrt(sq_ref[p] + EPSILON)
        coef = mag_ref[p] * inverse
        cd = coef * stat_ref[p] * (inverse * inverse)
        cd_ref[p] = cd
        g = g_keep[p].astype(F32) + g_got[p].astype(F32)
        ad = ad_keep[p].astype(F32) + ad_got[p].astype(F32)
        totals.append(coef * g - cd * ad)
    for i, j in enumerate(range(0, n, 2)):
        at = [block_at(n, order).index(j) * rows for order in orders]
        both = [totals[p][at[p] : at[p] + rows] for p in range(2)]
        blocks[i][...] = jnp.concatenate(both, axis=0).astype(blocks[i].dtype)


def fold_call(n, orders, ad_keep, ad_got, g_keep, g_got, sq, stat, mag):
    _, half, width = ad_keep.shape
    tile = tile_of(width, 1792)
    rows = half * 4 // n
    big = pl.BlockSpec((2, half, tile), lambda f: (0, 0, f))
    line = pl.BlockSpec((2, 1, tile), lambda f: (0, 0, f))
    return pl.pallas_call(
        functools.partial(fold_kernel, n, orders),
        grid=(width // tile,),
        in_specs=[big] * 4 + [line] * 3,
        out_specs=[line] + [pl.BlockSpec((rows, tile), lambda f: (0, f))] * (n // 2),
        out_shape=[jax.ShapeDtypeStruct((2, 1, width), F32)]
        + [jax.ShapeDtypeStruct((rows, width), F32 if j == 0 else BF) for j in range(n // 2)],
        compiler_params=params(),
        name="fold_rows",
    )(ad_keep, ad_got, g_keep, g_got, sq, stat, mag)


def order_kernel(n, orders, has_prior, me_ref, low_ref, high_ref, *refs):
    out_ref = refs[-1]
    rank = out_ref.shape[1]
    for p in range(2):
        choice = row_choice(n, rank // n, me_ref[0], orders[p], transpose=True)
        both = jnp.concatenate([low_ref[p], high_ref[p]], axis=0)
        out_ref[p] = dot(choice, both)


def order_call(n, orders, me, low, high, prior, first, width):
    _, half, size = low.shape
    tile = tile_of(math.gcd(first, size), 3584)
    start = first // tile
    args = [me, low, high]
    specs = [
        pl.BlockSpec(memory_space=pltpu.SMEM),
        pl.BlockSpec((2, half, tile), lambda f: (0, 0, f)),
        pl.BlockSpec((2, half, tile), lambda f: (0, 0, f)),
    ]
    aliases = {}
    if prior is not None:
        aliases = {3: 0}
        args.append(prior)
        specs.append(pl.BlockSpec(memory_space=pl.ANY))
    return pl.pallas_call(
        functools.partial(order_kernel, n, orders, prior is not None),
        grid=(size // tile,),
        in_specs=specs,
        out_specs=pl.BlockSpec((2, 2 * half, tile), lambda f: (0, 0, f + start)),
        out_shape=jax.ShapeDtypeStruct((2, 2 * half, width), F32),
        input_output_aliases=aliases,
        compiler_params=params(),
        name="order_rows",
    )(*args)


def tied(*xs):
    return lax.optimization_barrier(xs)


class Turn:
    def __init__(self, token):
        self.token = token

    def pass_on(self, *xs):
        self.token, *xs = tied(self.token, *xs)
        return tuple(xs)


class Halving:
    def __init__(self, orders, keep, send, dtype=BF):
        self.flat = keep.ndim == 2
        self.orders, self.dtype = orders[:1] if self.flat else orders, dtype
        self.parts = [(keep,) if self.flat else (keep[0], keep[1])]
        self.whole = [keep]
        self.send, self.step, self.rows = [send], 0, keep.shape[0 if self.flat else 1]

    def sums(self, low, high):
        return [sum(part[p][low:high].astype(F32) for part in self.parts) for p in range(len(self.orders))]

    def prepare(self):
        if self.step:
            self.rows //= 2
            self.send = [x.astype(self.dtype) for x in self.sums(self.rows, 2 * self.rows)]
        return self.send

    def go(self, send):
        if self.step:
            self.got = [swap(x, "col", order[self.step]) for x, order in zip(send, self.orders)]
        else:
            self.got = [swap(send[0], "col", self.orders[0][0])]
        return self.got

    def arrived(self, got):
        if self.step or self.flat:
            self.parts.append(tuple(got))
            self.whole.append(tuple(got) if len(got) > 1 else got[0])
        else:
            self.parts.append((got[0][0], got[0][1]))
            self.whole.append(got[0])
        self.step += 1

    def done(self):
        return self.step == len(self.orders[0])

    def own(self):
        return self.sums(0, self.rows)

    def pairs(self):
        return [x if isinstance(x, tuple) else (x, x) for x in self.whole]


class Lanes:
    def __init__(self, bits, squares, xa):
        self.bits, self.squares, self.xa = bits, squares, xa

    def prepare(self):
        return [jnp.concatenate([self.squares, *self.xa.prepare()], axis=0)]

    def go(self, send):
        return [swap(send[0], "col", self.bits[self.xa.step])]

    def arrived(self, got):
        rows = self.squares.shape[0]
        self.squares = self.squares + got[0][:rows]
        self.xa.arrived([got[0][rows:]])

    def done(self):
        return self.xa.done()


class Statistic:
    def __init__(self, n, stat, u):
        self.n, self.stat, self.u, self.step = n, stat, u, 0

    def prepare(self):
        both = jnp.concatenate([self.stat, self.u], axis=0)
        return [both.astype(BF) if self.step else both]

    def go(self, send):
        return [swap(send[0], "col", j) for j in ([1], range(2, self.n, 2))[self.step]]

    def arrived(self, got):
        rows = self.stat.shape[0]
        self.stat = self.stat + sum(x[:rows].astype(F32) for x in got)
        self.u = jnp.concatenate([self.u] + [x[rows:].astype(F32) for x in got], axis=0)
        self.step += 1

    def done(self):
        return self.step == 2


class First:
    def __init__(self, send):
        self.send, self.got = send, None

    def prepare(self):
        return [self.send]

    def go(self, send):
        return [swap(send[0], "col", 1)]

    def arrived(self, got):
        self.got = got[0]

    def done(self):
        return self.got is not None


class Scattering:
    def __init__(self, n, blocks):
        self.n, self.blocks, self.own = n, blocks, None

    def prepare(self):
        return self.blocks[1:]

    def go(self, send):
        return [swap(x, "col", j) for x, j in zip(send, range(2, self.n, 2))]

    def arrived(self, got):
        total = sum(x.astype(F32) for x in [self.blocks[0], *got])
        rows = total.shape[0] // 2
        self.own = [total[p * rows : (p + 1) * rows].astype(BF) for p in range(2)]

    def done(self):
        return self.own is not None


class Laying:
    def __init__(self, orders, own):
        self.orders, self.held, self.step = orders, own, len(orders[0]) - 1

    def prepare(self):
        return self.held if self.step else [jnp.stack(self.held)]

    def go(self, send):
        self.held = list(send)
        if self.step:
            return [swap(x, "col", order[self.step]) for x, order in zip(send, self.orders)]
        return [swap(send[0], "col", self.orders[0][0])]

    def arrived(self, got):
        if self.step:
            self.held = [jnp.concatenate(pair, axis=0) for pair in zip(self.held, got)]
        else:
            self.held += list(got)
        self.step -= 1

    def done(self):
        return self.step < 0


class Around:
    def __init__(self, n, xs):
        self.n, self.xs, self.got = n, xs, None

    def prepare(self):
        return self.xs

    def go(self, send):
        return [swap(x, "row", k) for k, x in enumerate(send, start=1)]

    def arrived(self, got):
        self.got = list(got)

    def done(self):
        return self.got is not None


def phase(turn, moves, kernel=None, late=(), ready=()):
    moves = [move for move in moves if not move.done()]
    late = [move for move in late if not move.done()]
    ready = [move for move in ready if not move.done()]
    sends = [move.prepare() for move in moves + late]
    sent = list(turn.pass_on(*[x for send in sends for x in send]))
    got = [move.go([sent.pop(0) for _ in send]) for move, send in zip(moves + late, sends)]
    for move, g in zip(late, got[len(moves) :]):
        move.pending = g
    waited = moves + ready
    got = got[: len(moves)] + [move.pending for move in ready]
    outs = kernel(turn.token) if kernel else ()
    flat = list(turn.pass_on(*[x for g in got for x in g], *outs))
    for move, g in zip(waited, got):
        move.arrived([flat.pop(0) for _ in g])
    return flat


def on_device(tokens, weights, adapter_in, adapter_out, magnitude, hidden_cot):
    n, n_row = lax.axis_size("col"), lax.axis_size("row")
    rank = adapter_in.shape[1]
    share = hidden_cot.shape[0]
    width = weights.shape[2]
    orders = bit_orders(n)
    bits = orders[0]
    steps = len(bits)
    me = jnp.stack([lax.axis_index("col"), lax.axis_index("row")]).astype(jnp.int32)
    mag = magnitude[:, None, :]
    sizes = [width * q // sum(QUARTERS) for q in QUARTERS]
    firsts = [sum(sizes[:c]) for c in range(len(sizes))]
    count = len(sizes)

    xs = [tokens] + [swap(tokens, "row", k) for k in range(1, n_row)]
    ad_keep, ad_send, sq = adapter_call(n, orders, me, adapter_in, weights, adapter_out)
    turn = Turn(me)
    *xs, sq, ad_send = turn.pass_on(*xs, sq, ad_send)
    sq_first, ad_first = First(sq.reshape(-1, 128)), First(ad_send)

    def project(c):
        return lambda token: token_call(
            n, share, orders, token, xs, adapter_in, weights, adapter_out, firsts[c], sizes[c], c == 0
        )

    def elementwise(c):
        return lambda token: own_call(
            n, orders, token, share, halvings[c].pairs(), [x[0] for x in xa.parts], squares, mag, adapter_out,
            hidden_cot, hidden, firsts[c], sizes[c],
        )

    outs = phase(turn, [sq_first, ad_first], project(0))
    halvings = [Halving(orders, outs[0], outs[1])]
    xa = Halving(orders, outs[2], outs[3], F32)
    phase(turn, [xa, halvings[0]])
    lanes = Lanes(bits, sq_first.send + sq_first.got, xa)
    for c in range(1, count):
        outs = phase(turn, [lanes, halvings[c - 1]], project(c))
        halvings.append(Halving(orders, outs[0], outs[1]))
        phase(turn, [lanes, *halvings])
    hidden, results = None, []
    for c in range(count):
        while not (lanes.done() and halvings[c].done()):
            phase(turn, [lanes, halvings[c]])
        squares = lanes.squares.reshape(2, 1, -1)
        hidden, *outs = phase(turn, halvings[c + 1 : c + 2], elementwise(c))
        results.append(outs)
    g_keep, g_send = [jnp.concatenate([r[i] for r in results], axis=2) for i in range(2)]
    g_first = First(g_send)
    stat = jnp.concatenate([r[2] for r in results], axis=2).reshape(-1, 128)
    statistic = Statistic(n, stat, sum(r[3] for r in results))
    phase(turn, [statistic, g_first])
    phase(turn, [statistic])
    stat = statistic.stat.reshape(2, 1, -1)
    cd, *blocks = fold_call(n, orders, ad_keep, ad_first.got, g_keep, g_first.got, squares, stat, mag)
    scattering = Scattering(n, blocks)
    seconds = phase(
        turn,
        [scattering],
        lambda token: [second_call(weights, adapter_out, adapter_in, cd, 0, width, token)],
    )
    laying = Laying(orders, scattering.own)
    pieces = turn.pass_on(*join_call(share, bits[::-1], turn.token, xs, seconds, [statistic.u]))
    away = Around(n_row, pieces[1:])
    phase(turn, [laying, away])
    total = (pieces[0] + sum(x.astype(F32) for x in away.got)).astype(BF)
    back = Around(n_row, [total] * (n_row - 1))
    while laying.step or not back.done():
        phase(turn, [laying, back])
    (grad_in,) = phase(turn, [laying], lambda token: [lay_call(token, [total] + back.got)])
    low, high = laying.held
    grad_out = order_call(n, orders, turn.token, low, high, None, 0, width)
    grad_in = grad_in.reshape(2, -1, grad_in.shape[1])
    grad_mag = (stat / jnp.sqrt(squares + EPSILON))[:, 0, :]
    return (hidden, grad_in, grad_out, grad_mag)


def solution(mesh):
    in_specs = (
        P("row", "col"),
        P(None, "col", "row"),
        P(None, None, "col"),
        P(None, None, "row"),
        P(None, "row"),
        P("col", "row"),
    )
    out_specs = (P("col", "row"), P(None, None, "col"), P(None, None, "row"), P(None, "row"))
    return jax.shard_map(
        on_device, mesh=mesh, in_specs=in_specs, out_specs=out_specs, check_vma=False
    )
```

```python
import functools
import math

import jax
import jax.numpy as jnp
from jax import lax
from jax.experimental import pallas as pl
from jax.experimental.pallas import tpu as pltpu
from jax.sharding import PartitionSpec as P

EPSILON = 1e-06
QUARTERS = (2, 2)
SLOTS = 4
STEP = 1792
VMEM_LIMIT = 48 * 1024 * 1024
VMEM_REST = 30 * 1024 * 1024
VMEM_FIRST = 62 * 1024 * 1024
BF = jnp.bfloat16
F32 = jnp.float32


def tile_of(width, largest):
    for tile in (3584, 1792, 1024, 896, 512, 256, 128):
        if tile <= largest and width % tile == 0:
            return tile
    return width


def bit_orders(n):
    bits = [1 << i for i in range(n.bit_length() - 1)]
    return (bits, bits[:1] + bits[1:][::-1])


def block_at(n, order):
    steps = len(order)
    return [sum(order[i] for i in range(steps) if pos >> (steps - 1 - i) & 1) for pos in range(n)]


def swap(x, axis, bit):
    n = lax.axis_size(axis)
    return lax.ppermute(x, axis, [(i, i ^ bit) for i in range(n)])


def stream(w_ref, buf, sem, step, per, first):
    slots = buf.shape[0]
    ahead = max(slots - 2, 1)
    total = 2 * per
    at = pl.program_id(0) * per + pl.program_id(1)

    def copy(i):
        start = pl.multiple_of(first + (i % per) * step, step)
        return pltpu.make_async_copy(
            w_ref.at[i // per, :, pl.ds(start, step)], buf.at[i % slots], sem.at[i % slots]
        )

    @pl.when(at == 0)
    def _():
        for i in range(min(ahead, total)):
            copy(jnp.int32(i)).start()

    def wait():
        copy(at).wait()

        @pl.when(at + ahead < total)
        def _():
            copy(at + ahead).start()

    return buf.at[at % slots], wait


class Stream:
    def __init__(self, w_ref, buf, sem, step, per, first):
        self.w_ref, self.buf, self.sem = w_ref, buf, sem
        self.step, self.per, self.first = step, per, first
        self.slots, self.total = buf.shape[0], 2 * per
        self.ahead = max(self.slots - 2, 1)
        for i in range(min(self.ahead, self.total)):
            self.copy(jnp.int32(i)).start()

    def copy(self, i):
        start = pl.multiple_of(self.first + (i % self.per) * self.step, self.step)
        slot = i % self.slots
        return pltpu.make_async_copy(
            self.w_ref.at[i // self.per, :, pl.ds(start, self.step)], self.buf.at[slot], self.sem.at[slot]
        )

    def over(self, p, body):
        @pl.loop(0, self.per)
        def _(f):
            at = p * self.per + f
            self.copy(at).wait()

            @pl.when(at + self.ahead < self.total)
            def _():
                self.copy(at + self.ahead).start()

            start = pl.multiple_of(f * self.step, self.step)
            whole = pl.ds(pl.multiple_of(self.first + start, self.step), self.step)
            body(self.buf.at[at % self.slots], whole, pl.ds(start, self.step))


def stream_scratch(depth, step, total):
    slots = min(SLOTS, total + 1)
    return [pltpu.VMEM((slots, depth, step), BF), pltpu.SemaphoreType.DMA((slots,))]


def dot(a, b, dims=((1,), (0,))):
    return lax.dot_general(a, b, (dims, ((), ())), preferred_element_type=F32)


def split3(x):
    hi = x.astype(BF)
    rest = x - hi.astype(F32)
    mid = rest.astype(BF)
    return hi, mid, (rest - mid.astype(F32)).astype(BF)


def params(limit=VMEM_LIMIT):
    return pltpu.CompilerParams(vmem_limit_bytes=limit)


def row_choice(n_blocks, rows, me, order, transpose=False):
    size = n_blocks * rows
    dst = lax.broadcasted_iota(jnp.int32, (size, size), 1 if transpose else 0)
    src = lax.broadcasted_iota(jnp.int32, (size, size), 0 if transpose else 1)
    pos = dst // rows
    block = jnp.zeros_like(pos)
    steps = len(order)
    for i in range(steps):
        block = block + ((pos >> (steps - 1 - i)) & 1) * order[i]
    wanted = (block ^ me) * rows + dst % rows
    return (wanted == src).astype(F32).astype(BF)


def adapter_kernel(n, orders, step, per, me_ref, a_ref, w_ref, b_ref, keep_ref, send_ref, sq_ref, aperm, gram, buf, sem):
    rank = a_ref.shape[1]
    w_tile, wait = stream(w_ref, buf, sem, step, per, 0)

    @pl.when(pl.program_id(1) == 0)
    def _():
        for p in range(2):

            @pl.when(pl.program_id(0) == p)
            def _(p=p):
                choice = row_choice(n, rank // n, me_ref[0], orders[p])
                aperm[...] = dot(choice, a_ref[p]).astype(BF)
                for i, part in enumerate(split3(dot(aperm[...], a_ref[p], ((1,), (1,))))):
                    gram[:rank, i * rank : (i + 1) * rank] = part
                gram[rank:, :rank] = choice

        gram[rank:, rank:] = jnp.zeros((rank, 2 * rank), BF)

    wait()
    b = b_ref[0]
    aw = dot(aperm[...], w_tile[...])
    squares = jnp.zeros((8, step), F32)
    slab = 64
    for i in range(w_tile.shape[0] // slab):
        w = w_tile[i * slab : (i + 1) * slab, :].astype(F32)
        squares = squares + jnp.sum((w * w).reshape(slab // 8, 8, step), axis=0)
    both = dot(gram[...], jnp.concatenate([b, b, b], axis=0))
    ad = aw + both[:rank]
    keep_ref[0] = ad[: rank // 2].astype(BF)
    send_ref[0] = ad[rank // 2 :].astype(BF)
    cross = (aw + ad) * both[rank:]
    sq_ref[0] = jnp.sum(squares, axis=0, keepdims=True) + jnp.sum(cross, axis=0, keepdims=True)


def adapter_call(n, orders, me, a, w, b):
    _, depth, width = w.shape
    rank = a.shape[1]
    tile = tile_of(width, STEP)
    return pl.pallas_call(
        functools.partial(adapter_kernel, n, orders, tile, width // tile),
        grid=(2, width // tile),
        in_specs=[
            pl.BlockSpec(memory_space=pltpu.SMEM),
            pl.BlockSpec(a.shape, lambda p, f: (0, 0, 0)),
            pl.BlockSpec(memory_space=pl.ANY),
            pl.BlockSpec((1, rank, tile), lambda p, f: (p, 0, f)),
        ],
        out_specs=[
            pl.BlockSpec((1, rank // 2, tile), lambda p, f: (p, 0, f)),
            pl.BlockSpec((1, rank // 2, tile), lambda p, f: (p, 0, f)),
            pl.BlockSpec((1, 1, tile), lambda p, f: (p, 0, f)),
        ],
        out_shape=[
            jax.ShapeDtypeStruct((2, rank // 2, width), BF),
            jax.ShapeDtypeStruct((2, rank // 2, width), BF),
            jax.ShapeDtypeStruct((2, 1, width), F32),
        ],
        scratch_shapes=[pltpu.VMEM((rank, depth), BF), pltpu.VMEM((2 * rank, 3 * rank), BF)]
        + stream_scratch(depth, tile, 2 * (width // tile)),
        compiler_params=params(VMEM_FIRST),
        cost_estimate=pl.CostEstimate(
            flops=2 * 4 * rank * depth * width, bytes_accessed=w.size * 2, transcendentals=0
        ),
        name="adapter_pass",
    )(me, a, w, b)


def place_tokens(order, share, me, row, x_refs, x_all):
    steps = len(order)
    per = x_refs[0].shape[0] // share
    for k, x_ref in enumerate(x_refs):
        for h in range(per):
            block = ((row ^ k) * per + h) ^ me
            pos = jnp.int32(0)
            for i in range(steps):
                bit = order[i].bit_length() - 1
                pos = pos + (((block >> bit) & 1) << (steps - 1 - i))
            start = pl.multiple_of(pos * share, share)
            x_all[pl.ds(start, share), :] = x_ref[h * share : (h + 1) * share, :]


def token_kernel(n, share, orders, nx, emit_xa, step, per, first, me_ref, *refs):
    x_refs, (a_ref, w_ref, b_ref) = refs[:nx], refs[nx : nx + 3]
    outs = refs[nx + 3 :]
    keep_ref, send_ref = outs[:2]
    left, xa, buf, sem = outs[-4:]
    rank = a_ref.shape[1]
    rows = left.shape[0]
    half = rows // 2
    w_tile, wait = stream(w_ref, buf, sem, step, per, first)

    @pl.when(pl.program_id(1) == 0)
    def _():
        me, row = me_ref[0], me_ref[1]
        for p in range(2):

            @pl.when(pl.program_id(0) == p)
            def _(p=p):
                place_tokens(orders[p], share, me, row, x_refs, left)
                if emit_xa and p == 0:
                    both = dot(left[...], a_ref[...].reshape(2 * rank, -1), ((1,), (1,)))
                    outs[2][...] = both[:half]
                    outs[3][...] = both[half:]
                product = dot(left[...], a_ref[p], ((1,), (1,)))
                hi = product.astype(BF)
                xa[:, :rank] = hi
                xa[:, rank:] = (product - hi.astype(F32)).astype(BF)

    wait()
    b = b_ref[0]
    y = dot(left[...], w_tile[...]) + dot(xa[...], jnp.concatenate([b, b], axis=0))
    keep_ref[0] = y[:half].astype(BF)
    send_ref[0] = y[half:].astype(BF)


def token_call(n, share, orders, me, xs, a, w, b, first, size, emit_xa):
    _, depth, width = w.shape
    rank = a.shape[1]
    tile = tile_of(math.gcd(first, size), STEP)
    start = first // tile
    rows = n * share
    half = jax.ShapeDtypeStruct((2, rows // 2, size), BF)
    half_spec = pl.BlockSpec((1, rows // 2, tile), lambda p, f: (p, 0, f))
    out_shape, out_specs = [half, half], [half_spec, half_spec]
    if emit_xa:
        out_shape += [jax.ShapeDtypeStruct((rows // 2, 2 * rank), F32)] * 2
        out_specs += [pl.BlockSpec((rows // 2, 2 * rank), lambda p, f: (0, 0))] * 2
    return pl.pallas_call(
        functools.partial(token_kernel, n, share, orders, len(xs), emit_xa, tile, size // tile, first),
        grid=(2, size // tile),
        in_specs=[pl.BlockSpec(memory_space=pltpu.SMEM)]
        + [pl.BlockSpec(x.shape, lambda p, f: (0, 0)) for x in xs]
        + [
            pl.BlockSpec(a.shape, lambda p, f: (0, 0, 0)),
            pl.BlockSpec(memory_space=pl.ANY),
            pl.BlockSpec((1, rank, tile), lambda p, f: (p, 0, f + start)),
        ],
        out_specs=out_specs,
        out_shape=out_shape,
        scratch_shapes=[pltpu.VMEM((rows, depth), BF), pltpu.VMEM((rows, 2 * rank), BF)]
        + stream_scratch(depth, tile, 2 * (size // tile)),
        compiler_params=params(VMEM_LIMIT if emit_xa else VMEM_REST),
        cost_estimate=pl.CostEstimate(
            flops=4 * rows * depth * size, bytes_accessed=4 * depth * size, transcendentals=0
        ),
        name="token_pass",
    )(me, *xs, a, w, b)


def own_kernel(n, orders, n_parts, n_xa, has_prior, me_ref, *refs):
    y_refs = refs[: 2 * n_parts]
    xa_refs = refs[2 * n_parts : 2 * n_parts + n_xa]
    refs = refs[2 * n_parts + n_xa :]
    sq_ref, mag_ref, b_ref, cot_ref = refs[:4]
    outs = refs[4 + has_prior :]
    hid_ref, keep_ref, send_ref, stat_ref, ut_ref, xa = outs
    half = keep_ref.shape[1]
    ys, coefs = [], []
    for p in range(2):
        y = y_refs[p][0].astype(F32)
        for i in range(1, n_parts):
            part = y_refs[2 * i + p]
            y = y + (part[0] if len(part.shape) == 3 else part[...]).astype(F32)
        ys.append(y)
        coefs.append(mag_ref[p] * lax.rsqrt(sq_ref[p] + EPSILON))
    gate, up = ys[0] * coefs[0], ys[1] * coefs[1]
    sig = jax.nn.sigmoid(gate)
    cot = cot_ref[...].astype(F32)
    hid_ref[...] = (gate * sig * up).astype(BF)
    d_pre = (
        (cot * up * sig * (1.0 + gate * (1.0 - sig))).astype(BF),
        (cot * gate * sig).astype(BF),
    )

    @pl.when(pl.program_id(0) == 0)
    def _():
        ut_ref[...] = jnp.zeros_like(ut_ref)
        rank = xa.shape[2]
        product = xa_refs[0][...]
        for ref in xa_refs[1:]:
            product = product + ref[...]
        product = product.astype(BF)
        for p in range(2):
            choice = row_choice(n, rank // n, me_ref[0], orders[p])
            xa[p] = dot(product[:, p * rank : (p + 1) * rank], choice, ((1,), (1,))).astype(BF)

    for p in range(2):
        d = d_pre[p]
        stat_ref[p] = jnp.sum(d.astype(F32) * ys[p], axis=0, keepdims=True)
        ag = dot(xa[p], d, ((0,), (0,)))
        keep_ref[p] = ag[:half].astype(BF)
        send_ref[p] = ag[half:].astype(BF)
        scaled = (b_ref[p].astype(F32) * coefs[p]).astype(BF)
        rank = scaled.shape[0]
        ut_ref[:, p * rank : (p + 1) * rank] += dot(d, scaled, ((1,), (1,)))


def own_call(n, orders, me, share, parts, xas, sq, mag, b, cot, prior, first, size):
    width = b.shape[2]
    rank = b.shape[1]
    tile = tile_of(math.gcd(first, size), 3584)
    start = first // tile
    y_args, y_specs = [], []
    for pair in parts:
        for p in range(2):
            part = pair[p]
            y_args.append(part)
            if part.ndim == 3:
                y_specs.append(pl.BlockSpec((1, share, tile), functools.partial(lambda p, f: (p, 0, f), p)))
            else:
                y_specs.append(pl.BlockSpec((share, tile), lambda f: (0, f)))
    half = jax.ShapeDtypeStruct((2, rank // 2, size), BF)
    half_spec = pl.BlockSpec((2, rank // 2, tile), lambda f: (0, 0, f))
    args = [me, *y_args, *xas, sq, mag, b, cot]
    specs = [pl.BlockSpec(memory_space=pltpu.SMEM)] + y_specs
    specs += [pl.BlockSpec((share, x.shape[1]), lambda f: (0, 0)) for x in xas]
    specs += [
        pl.BlockSpec((2, 1, tile), lambda f: (0, 0, f + start)),
        pl.BlockSpec((2, 1, tile), lambda f: (0, 0, f + start)),
        pl.BlockSpec((2, rank, tile), lambda f: (0, 0, f + start)),
        pl.BlockSpec((share, tile), lambda f: (0, f + start)),
    ]
    aliases = {}
    if prior is not None:
        aliases = {len(args): 0}
        args.append(prior)
        specs.append(pl.BlockSpec(memory_space=pl.ANY))
    return pl.pallas_call(
        functools.partial(own_kernel, n, orders, len(parts), len(xas), prior is not None),
        grid=(size // tile,),
        in_specs=specs,
        out_specs=[
            pl.BlockSpec((share, tile), lambda f: (0, f + start)),
            half_spec,
            half_spec,
            pl.BlockSpec((2, 1, tile), lambda f: (0, 0, f)),
            pl.BlockSpec((share, 2 * rank), lambda f: (0, 0)),
        ],
        out_shape=[
            jax.ShapeDtypeStruct((share, width), BF),
            half,
            half,
            jax.ShapeDtypeStruct((2, 1, size), F32),
            jax.ShapeDtypeStruct((share, 2 * rank), F32),
        ],
        input_output_aliases=aliases,
        scratch_shapes=[pltpu.VMEM((2, share, rank), BF)],
        compiler_params=params(VMEM_REST),
        cost_estimate=pl.CostEstimate(
            flops=4 * rank * share * size * 2, bytes_accessed=share * size * 20, transcendentals=share * size
        ),
        name="own_tokens",
    )(*args)


def second_kernel(step, per, first, token_ref, w_ref, b_ref, a_ref, cd_ref, out_ref, small, buf, sem):
    tiles = Stream(w_ref, buf, sem, step, per, first)
    for p in range(2):
        out_ref[p] = jnp.zeros(out_ref.shape[1:], F32)
        small[...] = jnp.zeros_like(small)

        def body(w_tile, whole, _, p=p):
            b = b_ref[p, :, whole]
            scaled = (b.astype(F32) * cd_ref[p, :, whole]).astype(BF)
            out_ref[p] += dot(scaled, w_tile[...], ((1,), (1,)))
            small[...] += dot(scaled, b, ((1,), (1,)))

        tiles.over(p, body)
        parts = jnp.concatenate(split3(small[...]), axis=1)
        out_ref[p] += dot(parts, jnp.concatenate([a_ref[p]] * 3, axis=0))


def second_call(w, b, a, cd, first, size, token):
    _, depth, width = w.shape
    rank = b.shape[1]
    tile = tile_of(math.gcd(first, size), STEP)
    vmem = pl.BlockSpec(memory_space=pltpu.VMEM)
    return pl.pallas_call(
        functools.partial(second_kernel, tile, size // tile, first),
        in_specs=[pl.BlockSpec(memory_space=pltpu.SMEM), pl.BlockSpec(memory_space=pl.ANY), vmem, vmem, vmem],
        out_specs=vmem,
        out_shape=jax.ShapeDtypeStruct((2, rank, depth), F32),
        scratch_shapes=[pltpu.VMEM((rank, rank), F32)] + stream_scratch(depth, tile, 2 * (size // tile)),
        compiler_params=params(VMEM_REST),
        cost_estimate=pl.CostEstimate(
            flops=4 * rank * depth * size, bytes_accessed=4 * depth * size, transcendentals=0
        ),
        name="second_pass",
    )(token, w, b, a, cd)


def join_kernel(share, order, nx, nc, me_ref, *refs):
    x_refs, seconds, ut_refs = refs[:nx], refs[nx : nx + nc], refs[nx + nc : -(nx + 2)]
    outs, (x_all, total) = refs[-(nx + 2) : -2], refs[-2:]
    me, row = me_ref[0], me_ref[1]
    place_tokens(order, share, me, row, x_refs, x_all)
    rank = total.shape[0] // 2
    x = x_all[...]
    for p in range(2):
        ut = ut_refs[0][:, p * rank : (p + 1) * rank].astype(BF)
        away = seconds[0][p]
        for second in seconds[1:]:
            away = away + second[p]
        total[p * rank : (p + 1) * rank, :] = dot(ut, x, ((0,), (0,))) - away
    piece = 2 * rank // nx
    for k in range(nx):
        start = pl.multiple_of((row ^ k) * piece, piece)
        outs[k][...] = total[pl.ds(start, piece), :].astype(outs[k].dtype)


def join_call(share, order, me, xs, seconds, uts):
    depth = xs[0].shape[1]
    rank = seconds[0].shape[1]
    nx = len(xs)
    rows = sum(x.shape[0] for x in xs)
    piece = 2 * rank // nx
    vmem = pl.BlockSpec(memory_space=pltpu.VMEM)
    return pl.pallas_call(
        functools.partial(join_kernel, share, order, nx, len(seconds)),
        in_specs=[pl.BlockSpec(memory_space=pltpu.SMEM)] + [vmem] * (nx + len(seconds) + len(uts)),
        out_specs=[vmem] * nx,
        out_shape=[jax.ShapeDtypeStruct((piece, depth), F32 if k == 0 else BF) for k in range(nx)],
        scratch_shapes=[pltpu.VMEM((rows, depth), BF), pltpu.VMEM((2 * rank, depth), F32)],
        compiler_params=params(VMEM_REST),
        name="join_grad_in",
    )(me, *xs, *seconds, *uts)


def lay_kernel(me_ref, *refs):
    out_ref = refs[-1]
    row = me_ref[1]
    for k, ref in enumerate(refs[:-1]):
        piece = ref.shape[0]
        start = pl.multiple_of((row ^ k) * piece, piece)
        out_ref[pl.ds(start, piece), :] = ref[...].astype(F32)


def lay_call(me, pieces):
    rows = sum(x.shape[0] for x in pieces)
    vmem = pl.BlockSpec(memory_space=pltpu.VMEM)
    return pl.pallas_call(
        lay_kernel,
        in_specs=[pl.BlockSpec(memory_space=pltpu.SMEM)] + [vmem] * len(pieces),
        out_specs=vmem,
        out_shape=jax.ShapeDtypeStruct((rows, pieces[0].shape[1]), F32),
        compiler_params=params(VMEM_REST),
        name="lay_grad_in",
    )(me, *pieces)


def fold_kernel(n, orders, *refs):
    (ad_keep, ad_got, g_keep, g_got, sq_ref, stat_ref, mag_ref), outs = refs[:7], refs[7:]
    cd_ref, blocks = outs[0], outs[1:]
    rows = g_keep.shape[1] * 2 // n
    totals = []
    for p in range(2):
        inverse = lax.rsqrt(sq_ref[p] + EPSILON)
        coef = mag_ref[p] * inverse
        cd = coef * stat_ref[p] * (inverse * inverse)
        cd_ref[p] = cd
        g = g_keep[p].astype(F32) + g_got[p].astype(F32)
        ad = ad_keep[p].astype(F32) + ad_got[p].astype(F32)
        totals.append(coef * g - cd * ad)
    for i, j in enumerate(range(0, n, 2)):
        at = [block_at(n, order).index(j) * rows for order in orders]
        both = [totals[p][at[p] : at[p] + rows] for p in range(2)]
        blocks[i][...] = jnp.concatenate(both, axis=0).astype(blocks[i].dtype)


def fold_call(n, orders, ad_keep, ad_got, g_keep, g_got, sq, stat, mag):
    _, half, width = ad_keep.shape
    tile = tile_of(width, 1792)
    rows = half * 4 // n
    big = pl.BlockSpec((2, half, tile), lambda f: (0, 0, f))
    line = pl.BlockSpec((2, 1, tile), lambda f: (0, 0, f))
    return pl.pallas_call(
        functools.partial(fold_kernel, n, orders),
        grid=(width // tile,),
        in_specs=[big] * 4 + [line] * 3,
        out_specs=[line] + [pl.BlockSpec((rows, tile), lambda f: (0, f))] * (n // 2),
        out_shape=[jax.ShapeDtypeStruct((2, 1, width), F32)]
        + [jax.ShapeDtypeStruct((rows, width), F32 if j == 0 else BF) for j in range(n // 2)],
        compiler_params=params(VMEM_REST),
        name="fold_rows",
    )(ad_keep, ad_got, g_keep, g_got, sq, stat, mag)


def order_kernel(n, orders, has_prior, me_ref, low_ref, high_ref, *refs):
    out_ref = refs[-1]
    rank = out_ref.shape[1]
    for p in range(2):
        choice = row_choice(n, rank // n, me_ref[0], orders[p], transpose=True)
        both = jnp.concatenate([low_ref[p], high_ref[p]], axis=0)
        out_ref[p] = dot(choice, both)


def order_call(n, orders, me, low, high, prior, first, width):
    _, half, size = low.shape
    tile = tile_of(math.gcd(first, size), 3584)
    start = first // tile
    args = [me, low, high]
    specs = [
        pl.BlockSpec(memory_space=pltpu.SMEM),
        pl.BlockSpec((2, half, tile), lambda f: (0, 0, f)),
        pl.BlockSpec((2, half, tile), lambda f: (0, 0, f)),
    ]
    aliases = {}
    if prior is not None:
        aliases = {3: 0}
        args.append(prior)
        specs.append(pl.BlockSpec(memory_space=pl.ANY))
    return pl.pallas_call(
        functools.partial(order_kernel, n, orders, prior is not None),
        grid=(size // tile,),
        in_specs=specs,
        out_specs=pl.BlockSpec((2, 2 * half, tile), lambda f: (0, 0, f + start)),
        out_shape=jax.ShapeDtypeStruct((2, 2 * half, width), F32),
        input_output_aliases=aliases,
        compiler_params=params(VMEM_REST),
        name="order_rows",
    )(*args)


def tied(*xs):
    return lax.optimization_barrier(xs)


class Turn:
    def __init__(self, token):
        self.token = token

    def pass_on(self, *xs):
        self.token, *xs = tied(self.token, *xs)
        return tuple(xs)


class Halving:
    def __init__(self, orders, keep, send, dtype=BF):
        self.flat = keep.ndim == 2
        self.orders, self.dtype = orders[:1] if self.flat else orders, dtype
        self.parts = [(keep,) if self.flat else (keep[0], keep[1])]
        self.whole = [keep]
        self.send, self.step, self.rows = [send], 0, keep.shape[0 if self.flat else 1]

    def sums(self, low, high):
        return [sum(part[p][low:high].astype(F32) for part in self.parts) for p in range(len(self.orders))]

    def prepare(self):
        if self.step:
            self.rows //= 2
            self.send = [x.astype(self.dtype) for x in self.sums(self.rows, 2 * self.rows)]
        return self.send

    def go(self, send):
        if self.step:
            self.got = [swap(x, "col", order[self.step]) for x, order in zip(send, self.orders)]
        else:
            self.got = [swap(send[0], "col", self.orders[0][0])]
        return self.got

    def arrived(self, got):
        if self.step or self.flat:
            self.parts.append(tuple(got))
            self.whole.append(tuple(got) if len(got) > 1 else got[0])
        else:
            self.parts.append((got[0][0], got[0][1]))
            self.whole.append(got[0])
        self.step += 1

    def done(self):
        return self.step == len(self.orders[0])

    def own(self):
        return self.sums(0, self.rows)

    def pairs(self):
        return [x if isinstance(x, tuple) else (x, x) for x in self.whole]


class Lanes:
    def __init__(self, bits, squares, xa):
        self.bits, self.squares, self.xa = bits, squares, xa

    def prepare(self):
        return [jnp.concatenate([self.squares, *self.xa.prepare()], axis=0)]

    def go(self, send):
        return [swap(send[0], "col", self.bits[self.xa.step])]

    def arrived(self, got):
        rows = self.squares.shape[0]
        self.squares = self.squares + got[0][:rows]
        self.xa.arrived([got[0][rows:]])

    def done(self):
        return self.xa.done()


class Statistic:
    def __init__(self, n, stat, u):
        self.n, self.stat, self.u, self.step = n, stat, u, 0

    def prepare(self):
        both = jnp.concatenate([self.stat, self.u], axis=0)
        return [both.astype(BF) if self.step else both]

    def go(self, send):
        return [swap(send[0], "col", j) for j in ([1], range(2, self.n, 2))[self.step]]

    def arrived(self, got):
        rows = self.stat.shape[0]
        self.stat = self.stat + sum(x[:rows].astype(F32) for x in got)
        self.u = jnp.concatenate([self.u] + [x[rows:].astype(F32) for x in got], axis=0)
        self.step += 1

    def done(self):
        return self.step == 2


class First:
    def __init__(self, send):
        self.send, self.got = send, None

    def prepare(self):
        return [self.send]

    def go(self, send):
        return [swap(send[0], "col", 1)]

    def arrived(self, got):
        self.got = got[0]

    def done(self):
        return self.got is not None


class Scattering:
    def __init__(self, n, blocks):
        self.n, self.blocks, self.own = n, blocks, None

    def prepare(self):
        return self.blocks[1:]

    def go(self, send):
        return [swap(x, "col", j) for x, j in zip(send, range(2, self.n, 2))]

    def arrived(self, got):
        total = sum(x.astype(F32) for x in [self.blocks[0], *got])
        rows = total.shape[0] // 2
        self.own = [total[p * rows : (p + 1) * rows].astype(BF) for p in range(2)]

    def done(self):
        return self.own is not None


class Laying:
    def __init__(self, orders, own):
        self.orders, self.held, self.step = orders, own, len(orders[0]) - 1

    def prepare(self):
        return self.held if self.step else [jnp.stack(self.held)]

    def go(self, send):
        self.held = list(send)
        if self.step:
            return [swap(x, "col", order[self.step]) for x, order in zip(send, self.orders)]
        return [swap(send[0], "col", self.orders[0][0])]

    def arrived(self, got):
        if self.step:
            self.held = [jnp.concatenate(pair, axis=0) for pair in zip(self.held, got)]
        else:
            self.held += list(got)
        self.step -= 1

    def done(self):
        return self.step < 0


class Around:
    def __init__(self, n, xs):
        self.n, self.xs, self.got = n, xs, None

    def prepare(self):
        return self.xs

    def go(self, send):
        return [swap(x, "row", k) for k, x in enumerate(send, start=1)]

    def arrived(self, got):
        self.got = list(got)

    def done(self):
        return self.got is not None


def phase(turn, moves, kernel=None, late=(), ready=()):
    moves = [move for move in moves if not move.done()]
    late = [move for move in late if not move.done()]
    ready = [move for move in ready if not move.done()]
    sends = [move.prepare() for move in moves + late]
    sent = list(turn.pass_on(*[x for send in sends for x in send]))
    got = [move.go([sent.pop(0) for _ in send]) for move, send in zip(moves + late, sends)]
    for move, g in zip(late, got[len(moves) :]):
        move.pending = g
    waited = moves + ready
    got = got[: len(moves)] + [move.pending for move in ready]
    outs = kernel(turn.token) if kernel else ()
    flat = list(turn.pass_on(*[x for g in got for x in g], *outs))
    for move, g in zip(waited, got):
        move.arrived([flat.pop(0) for _ in g])
    return flat


def on_device(tokens, weights, adapter_in, adapter_out, magnitude, hidden_cot):
    n, n_row = lax.axis_size("col"), lax.axis_size("row")
    rank = adapter_in.shape[1]
    share = hidden_cot.shape[0]
    width = weights.shape[2]
    orders = bit_orders(n)
    bits = orders[0]
    steps = len(bits)
    me = jnp.stack([lax.axis_index("col"), lax.axis_index("row")]).astype(jnp.int32)
    mag = magnitude[:, None, :]
    sizes = [width * q // sum(QUARTERS) for q in QUARTERS]
    firsts = [sum(sizes[:c]) for c in range(len(sizes))]
    count = len(sizes)

    xs = [tokens] + [swap(tokens, "row", k) for k in range(1, n_row)]
    ad_keep, ad_send, sq = adapter_call(n, orders, me, adapter_in, weights, adapter_out)
    turn = Turn(me)
    *xs, sq, ad_send = turn.pass_on(*xs, sq, ad_send)
    sq_first, ad_first = First(sq.reshape(-1, 128)), First(ad_send)

    def project(c):
        return lambda token: token_call(
            n, share, orders, token, xs, adapter_in, weights, adapter_out, firsts[c], sizes[c], c == 0
        )

    def elementwise(c):
        return lambda token: own_call(
            n, orders, token, share, halvings[c].pairs(), [x[0] for x in xa.parts], squares, mag, adapter_out,
            hidden_cot, hidden, firsts[c], sizes[c],
        )

    outs = phase(turn, [sq_first, ad_first], project(0))
    halvings = [Halving(orders, outs[0], outs[1])]
    xa = Halving(orders, outs[2], outs[3], F32)
    phase(turn, [xa, halvings[0]])
    lanes = Lanes(bits, sq_first.send + sq_first.got, xa)
    for c in range(1, count):
        outs = phase(turn, [lanes, halvings[c - 1]], project(c))
        halvings.append(Halving(orders, outs[0], outs[1]))
        phase(turn, [lanes, *halvings])
    hidden, results = None, []
    for c in range(count):
        while not (lanes.done() and halvings[c].done()):
            phase(turn, [lanes, halvings[c]])
        squares = lanes.squares.reshape(2, 1, -1)
        hidden, *outs = phase(turn, halvings[c + 1 : c + 2], elementwise(c))
        results.append(outs)
    g_keep, g_send = [jnp.concatenate([r[i] for r in results], axis=2) for i in range(2)]
    g_first = First(g_send)
    stat = jnp.concatenate([r[2] for r in results], axis=2).reshape(-1, 128)
    statistic = Statistic(n, stat, sum(r[3] for r in results))
    phase(turn, [statistic, g_first])
    phase(turn, [statistic])
    stat = statistic.stat.reshape(2, 1, -1)
    cd, *blocks = fold_call(n, orders, ad_keep, ad_first.got, g_keep, g_first.got, squares, stat, mag)
    scattering = Scattering(n, blocks)
    seconds = phase(
        turn,
        [scattering],
        lambda token: [second_call(weights, adapter_out, adapter_in, cd, 0, width, token)],
    )
    laying = Laying(orders, scattering.own)
    pieces = turn.pass_on(*join_call(share, bits[::-1], turn.token, xs, seconds, [statistic.u]))
    away = Around(n_row, pieces[1:])
    phase(turn, [laying, away])
    total = (pieces[0] + sum(x.astype(F32) for x in away.got)).astype(BF)
    back = Around(n_row, [total] * (n_row - 1))
    while laying.step or not back.done():
        phase(turn, [laying, back])
    (grad_in,) = phase(turn, [laying], lambda token: [lay_call(token, [total] + back.got)])
    low, high = laying.held
    grad_out = order_call(n, orders, turn.token, low, high, None, 0, width)
    grad_in = grad_in.reshape(2, -1, grad_in.shape[1])
    grad_mag = (stat / jnp.sqrt(squares + EPSILON))[:, 0, :]
    return (hidden, grad_in, grad_out, grad_mag)


def solution(mesh):
    in_specs = (
        P("row", "col"),
        P(None, "col", "row"),
        P(None, None, "col"),
        P(None, None, "row"),
        P(None, "row"),
        P("col", "row"),
    )
    out_specs = (P("col", "row"), P(None, None, "col"), P(None, None, "row"), P(None, "row"))
    return jax.shard_map(
        on_device, mesh=mesh, in_specs=in_specs, out_specs=out_specs, check_vma=False
    )
```

```python
import functools
import math

import jax
import jax.numpy as jnp
from jax import lax
from jax.experimental import pallas as pl
from jax.experimental.pallas import tpu as pltpu
from jax.sharding import PartitionSpec as P

EPSILON = 1e-06
QUARTERS = (2, 2)
SLOTS = 4
STEP = 1792
VMEM_LIMIT = 48 * 1024 * 1024
VMEM_REST = 30 * 1024 * 1024
VMEM_FIRST = 62 * 1024 * 1024
BF = jnp.bfloat16
F32 = jnp.float32


def tile_of(width, largest):
    for tile in (3584, 1792, 1024, 896, 512, 256, 128):
        if tile <= largest and width % tile == 0:
            return tile
    return width


def bit_orders(n):
    bits = [1 << i for i in range(n.bit_length() - 1)]
    return (bits, bits[:1] + bits[1:][::-1])


def block_at(n, order):
    steps = len(order)
    return [sum(order[i] for i in range(steps) if pos >> (steps - 1 - i) & 1) for pos in range(n)]


def swap(x, axis, bit):
    n = lax.axis_size(axis)
    return lax.ppermute(x, axis, [(i, i ^ bit) for i in range(n)])


def stream(w_ref, buf, sem, step, per, first):
    slots = buf.shape[0]
    ahead = max(slots - 2, 1)
    total = 2 * per
    at = pl.program_id(0) * per + pl.program_id(1)

    def copy(i):
        start = pl.multiple_of(first + (i % per) * step, step)
        return pltpu.make_async_copy(
            w_ref.at[i // per, :, pl.ds(start, step)], buf.at[i % slots], sem.at[i % slots]
        )

    @pl.when(at == 0)
    def _():
        for i in range(min(ahead, total)):
            copy(jnp.int32(i)).start()

    def wait():
        copy(at).wait()

        @pl.when(at + ahead < total)
        def _():
            copy(at + ahead).start()

    return buf.at[at % slots], wait


class Stream:
    def __init__(self, w_ref, buf, sem, step, per, first):
        self.w_ref, self.buf, self.sem = w_ref, buf, sem
        self.step, self.per, self.first = step, per, first
        self.slots, self.total = buf.shape[0], 2 * per
        self.ahead = max(self.slots - 2, 1)
        for i in range(min(self.ahead, self.total)):
            self.copy(jnp.int32(i)).start()

    def copy(self, i):
        start = pl.multiple_of(self.first + (i % self.per) * self.step, self.step)
        slot = i % self.slots
        return pltpu.make_async_copy(
            self.w_ref.at[i // self.per, :, pl.ds(start, self.step)], self.buf.at[slot], self.sem.at[slot]
        )

    def over(self, p, body):
        @pl.loop(0, self.per)
        def _(f):
            at = p * self.per + f
            self.copy(at).wait()

            @pl.when(at + self.ahead < self.total)
            def _():
                self.copy(at + self.ahead).start()

            start = pl.multiple_of(f * self.step, self.step)
            whole = pl.ds(pl.multiple_of(self.first + start, self.step), self.step)
            body(self.buf.at[at % self.slots], whole, pl.ds(start, self.step))


def stream_scratch(depth, step, total):
    slots = min(SLOTS, total + 1)
    return [pltpu.VMEM((slots, depth, step), BF), pltpu.SemaphoreType.DMA((slots,))]


def dot(a, b, dims=((1,), (0,))):
    return lax.dot_general(a, b, (dims, ((), ())), preferred_element_type=F32)


def split3(x):
    hi = x.astype(BF)
    rest = x - hi.astype(F32)
    mid = rest.astype(BF)
    return hi, mid, (rest - mid.astype(F32)).astype(BF)


def params(limit=VMEM_LIMIT):
    return pltpu.CompilerParams(vmem_limit_bytes=limit)


def row_choice(n_blocks, rows, me, order, transpose=False):
    size = n_blocks * rows
    dst = lax.broadcasted_iota(jnp.int32, (size, size), 1 if transpose else 0)
    src = lax.broadcasted_iota(jnp.int32, (size, size), 0 if transpose else 1)
    pos = dst // rows
    block = jnp.zeros_like(pos)
    steps = len(order)
    for i in range(steps):
        block = block + ((pos >> (steps - 1 - i)) & 1) * order[i]
    wanted = (block ^ me) * rows + dst % rows
    return (wanted == src).astype(F32).astype(BF)


def adapter_kernel(n, orders, step, per, me_ref, a_ref, w_ref, b_ref, keep_ref, send_ref, sq_ref, aperm, gram, buf, sem):
    rank = a_ref.shape[1]
    w_tile, wait = stream(w_ref, buf, sem, step, per, 0)

    @pl.when(pl.program_id(1) == 0)
    def _():
        for p in range(2):

            @pl.when(pl.program_id(0) == p)
            def _(p=p):
                choice = row_choice(n, rank // n, me_ref[0], orders[p])
                aperm[...] = dot(choice, a_ref[p]).astype(BF)
                for i, part in enumerate(split3(dot(aperm[...], a_ref[p], ((1,), (1,))))):
                    gram[:rank, i * rank : (i + 1) * rank] = part
                gram[rank:, :rank] = choice

        gram[rank:, rank:] = jnp.zeros((rank, 2 * rank), BF)

    wait()
    b = b_ref[0]
    aw = dot(aperm[...], w_tile[...])
    squares = jnp.zeros((8, step), F32)
    slab = 64
    for i in range(w_tile.shape[0] // slab):
        w = w_tile[i * slab : (i + 1) * slab, :].astype(F32)
        squares = squares + jnp.sum((w * w).reshape(slab // 8, 8, step), axis=0)
    both = dot(gram[...], jnp.concatenate([b, b, b], axis=0))
    ad = aw + both[:rank]
    keep_ref[0] = ad[: rank // 2].astype(BF)
    send_ref[0] = ad[rank // 2 :].astype(BF)
    cross = (aw + ad) * both[rank:]
    sq_ref[0] = jnp.sum(squares, axis=0, keepdims=True) + jnp.sum(cross, axis=0, keepdims=True)


def adapter_call(n, orders, me, a, w, b):
    _, depth, width = w.shape
    rank = a.shape[1]
    tile = tile_of(width, STEP)
    return pl.pallas_call(
        functools.partial(adapter_kernel, n, orders, tile, width // tile),
        grid=(2, width // tile),
        in_specs=[
            pl.BlockSpec(memory_space=pltpu.SMEM),
            pl.BlockSpec(a.shape, lambda p, f: (0, 0, 0)),
            pl.BlockSpec(memory_space=pl.ANY),
            pl.BlockSpec((1, rank, tile), lambda p, f: (p, 0, f)),
        ],
        out_specs=[
            pl.BlockSpec((1, rank // 2, tile), lambda p, f: (p, 0, f)),
            pl.BlockSpec((1, rank // 2, tile), lambda p, f: (p, 0, f)),
            pl.BlockSpec((1, 1, tile), lambda p, f: (p, 0, f)),
        ],
        out_shape=[
            jax.ShapeDtypeStruct((2, rank // 2, width), BF),
            jax.ShapeDtypeStruct((2, rank // 2, width), BF),
            jax.ShapeDtypeStruct((2, 1, width), F32),
        ],
        scratch_shapes=[pltpu.VMEM((rank, depth), BF), pltpu.VMEM((2 * rank, 3 * rank), BF)]
        + stream_scratch(depth, tile, 2 * (width // tile)),
        compiler_params=params(VMEM_FIRST),
        cost_estimate=pl.CostEstimate(
            flops=2 * 4 * rank * depth * width, bytes_accessed=w.size * 2, transcendentals=0
        ),
        name="adapter_pass",
    )(me, a, w, b)


def place_tokens(order, share, me, row, x_refs, x_all):
    steps = len(order)
    per = x_refs[0].shape[0] // share
    for k, x_ref in enumerate(x_refs):
        for h in range(per):
            block = ((row ^ k) * per + h) ^ me
            pos = jnp.int32(0)
            for i in range(steps):
                bit = order[i].bit_length() - 1
                pos = pos + (((block >> bit) & 1) << (steps - 1 - i))
            start = pl.multiple_of(pos * share, share)
            x_all[pl.ds(start, share), :] = x_ref[h * share : (h + 1) * share, :]


def token_kernel(n, share, orders, nx, emit_xa, step, per, first, me_ref, *refs):
    x_refs, (a_ref, w_ref, b_ref) = refs[:nx], refs[nx : nx + 3]
    outs = refs[nx + 3 :]
    keep_ref, send_ref = outs[:2]
    left, xa, buf, sem = outs[-4:]
    rank = a_ref.shape[1]
    rows = left.shape[0]
    half = rows // 2
    w_tile, wait = stream(w_ref, buf, sem, step, per, first)

    @pl.when(pl.program_id(1) == 0)
    def _():
        me, row = me_ref[0], me_ref[1]
        for p in range(2):

            @pl.when(pl.program_id(0) == p)
            def _(p=p):
                place_tokens(orders[p], share, me, row, x_refs, left)
                if emit_xa and p == 0:
                    both = dot(left[...], a_ref[...].reshape(2 * rank, -1), ((1,), (1,)))
                    outs[2][...] = both[:half]
                    outs[3][...] = both[half:]
                product = dot(left[...], a_ref[p], ((1,), (1,)))
                hi = product.astype(BF)
                xa[:, :rank] = hi
                xa[:, rank:] = (product - hi.astype(F32)).astype(BF)

    wait()
    b = b_ref[0]
    y = dot(left[...], w_tile[...]) + dot(xa[...], jnp.concatenate([b, b], axis=0))
    keep_ref[0] = y[:half].astype(BF)
    send_ref[0] = y[half:].astype(BF)


def token_call(n, share, orders, me, xs, a, w, b, first, size, emit_xa):
    _, depth, width = w.shape
    rank = a.shape[1]
    tile = tile_of(math.gcd(first, size), STEP)
    start = first // tile
    rows = n * share
    half = jax.ShapeDtypeStruct((2, rows // 2, size), BF)
    half_spec = pl.BlockSpec((1, rows // 2, tile), lambda p, f: (p, 0, f))
    out_shape, out_specs = [half, half], [half_spec, half_spec]
    if emit_xa:
        out_shape += [jax.ShapeDtypeStruct((rows // 2, 2 * rank), F32)] * 2
        out_specs += [pl.BlockSpec((rows // 2, 2 * rank), lambda p, f: (0, 0))] * 2
    return pl.pallas_call(
        functools.partial(token_kernel, n, share, orders, len(xs), emit_xa, tile, size // tile, first),
        grid=(2, size // tile),
        in_specs=[pl.BlockSpec(memory_space=pltpu.SMEM)]
        + [pl.BlockSpec(x.shape, lambda p, f: (0, 0)) for x in xs]
        + [
            pl.BlockSpec(a.shape, lambda p, f: (0, 0, 0)),
            pl.BlockSpec(memory_space=pl.ANY),
            pl.BlockSpec((1, rank, tile), lambda p, f: (p, 0, f + start)),
        ],
        out_specs=out_specs,
        out_shape=out_shape,
        scratch_shapes=[pltpu.VMEM((rows, depth), BF), pltpu.VMEM((rows, 2 * rank), BF)]
        + stream_scratch(depth, tile, 2 * (size // tile)),
        compiler_params=params(VMEM_LIMIT if emit_xa else VMEM_REST),
        cost_estimate=pl.CostEstimate(
            flops=4 * rows * depth * size, bytes_accessed=4 * depth * size, transcendentals=0
        ),
        name="token_pass",
    )(me, *xs, a, w, b)


def own_kernel(n, orders, n_parts, n_xa, has_prior, me_ref, *refs):
    y_refs = refs[: 2 * n_parts]
    xa_refs = refs[2 * n_parts : 2 * n_parts + n_xa]
    refs = refs[2 * n_parts + n_xa :]
    sq_ref, mag_ref, b_ref, cot_ref = refs[:4]
    outs = refs[4 + has_prior :]
    hid_ref, keep_ref, send_ref, stat_ref, ut_ref, xa = outs
    half = keep_ref.shape[1]
    ys, coefs = [], []
    for p in range(2):
        y = y_refs[p][0].astype(F32)
        for i in range(1, n_parts):
            part = y_refs[2 * i + p]
            y = y + (part[0] if len(part.shape) == 3 else part[...]).astype(F32)
        ys.append(y)
        coefs.append(mag_ref[p] * lax.rsqrt(sq_ref[p] + EPSILON))
    gate, up = ys[0] * coefs[0], ys[1] * coefs[1]
    sig = jax.nn.sigmoid(gate)
    cot = cot_ref[...].astype(F32)
    hid_ref[...] = (gate * sig * up).astype(BF)
    d_pre = (
        (cot * up * sig * (1.0 + gate * (1.0 - sig))).astype(BF),
        (cot * gate * sig).astype(BF),
    )

    @pl.when(pl.program_id(0) == 0)
    def _():
        ut_ref[...] = jnp.zeros_like(ut_ref)
        rank = xa.shape[2]
        product = xa_refs[0][...]
        for ref in xa_refs[1:]:
            product = product + ref[...]
        product = product.astype(BF)
        for p in range(2):
            choice = row_choice(n, rank // n, me_ref[0], orders[p])
            xa[p] = dot(product[:, p * rank : (p + 1) * rank], choice, ((1,), (1,))).astype(BF)

    for p in range(2):
        d = d_pre[p]
        stat_ref[p] = jnp.sum(d.astype(F32) * ys[p], axis=0, keepdims=True)
        ag = dot(xa[p], d, ((0,), (0,)))
        keep_ref[p] = ag[:half].astype(BF)
        send_ref[p] = ag[half:].astype(BF)
        scaled = (b_ref[p].astype(F32) * coefs[p]).astype(BF)
        rank = scaled.shape[0]
        ut_ref[:, p * rank : (p + 1) * rank] += dot(d, scaled, ((1,), (1,)))


def own_call(n, orders, me, share, parts, xas, sq, mag, b, cot, prior, first, size):
    width = b.shape[2]
    rank = b.shape[1]
    tile = tile_of(math.gcd(first, size), 3584)
    start = first // tile
    y_args, y_specs = [], []
    for pair in parts:
        for p in range(2):
            part = pair[p]
            y_args.append(part)
            if part.ndim == 3:
                y_specs.append(pl.BlockSpec((1, share, tile), functools.partial(lambda p, f: (p, 0, f), p)))
            else:
                y_specs.append(pl.BlockSpec((share, tile), lambda f: (0, f)))
    half = jax.ShapeDtypeStruct((2, rank // 2, size), BF)
    half_spec = pl.BlockSpec((2, rank // 2, tile), lambda f: (0, 0, f))
    args = [me, *y_args, *xas, sq, mag, b, cot]
    specs = [pl.BlockSpec(memory_space=pltpu.SMEM)] + y_specs
    specs += [pl.BlockSpec((share, x.shape[1]), lambda f: (0, 0)) for x in xas]
    specs += [
        pl.BlockSpec((2, 1, tile), lambda f: (0, 0, f + start)),
        pl.BlockSpec((2, 1, tile), lambda f: (0, 0, f + start)),
        pl.BlockSpec((2, rank, tile), lambda f: (0, 0, f + start)),
        pl.BlockSpec((share, tile), lambda f: (0, f + start)),
    ]
    aliases = {}
    if prior is not None:
        aliases = {len(args): 0}
        args.append(prior)
        specs.append(pl.BlockSpec(memory_space=pl.ANY))
    return pl.pallas_call(
        functools.partial(own_kernel, n, orders, len(parts), len(xas), prior is not None),
        grid=(size // tile,),
        in_specs=specs,
        out_specs=[
            pl.BlockSpec((share, tile), lambda f: (0, f + start)),
            half_spec,
            half_spec,
            pl.BlockSpec((2, 1, tile), lambda f: (0, 0, f)),
            pl.BlockSpec((share, 2 * rank), lambda f: (0, 0)),
        ],
        out_shape=[
            jax.ShapeDtypeStruct((share, width), BF),
            half,
            half,
            jax.ShapeDtypeStruct((2, 1, size), F32),
            jax.ShapeDtypeStruct((share, 2 * rank), F32),
        ],
        input_output_aliases=aliases,
        scratch_shapes=[pltpu.VMEM((2, share, rank), BF)],
        compiler_params=params(VMEM_REST),
        cost_estimate=pl.CostEstimate(
            flops=4 * rank * share * size * 2, bytes_accessed=share * size * 20, transcendentals=share * size
        ),
        name="own_tokens",
    )(*args)


def second_kernel(step, per, first, token_ref, w_ref, b_ref, a_ref, cd_ref, out_ref, small, buf, sem):
    tiles = Stream(w_ref, buf, sem, step, per, first)
    for p in range(2):
        out_ref[p] = jnp.zeros(out_ref.shape[1:], F32)
        small[...] = jnp.zeros_like(small)

        def body(w_tile, whole, _, p=p):
            b = b_ref[p, :, whole]
            scaled = (b.astype(F32) * cd_ref[p, :, whole]).astype(BF)
            out_ref[p] += dot(scaled, w_tile[...], ((1,), (1,)))
            small[...] += dot(scaled, b, ((1,), (1,)))

        tiles.over(p, body)
        parts = jnp.concatenate(split3(small[...]), axis=1)
        out_ref[p] += dot(parts, jnp.concatenate([a_ref[p]] * 3, axis=0))


def second_call(w, b, a, cd, first, size, token):
    _, depth, width = w.shape
    rank = b.shape[1]
    tile = tile_of(math.gcd(first, size), STEP)
    vmem = pl.BlockSpec(memory_space=pltpu.VMEM)
    return pl.pallas_call(
        functools.partial(second_kernel, tile, size // tile, first),
        in_specs=[pl.BlockSpec(memory_space=pltpu.SMEM), pl.BlockSpec(memory_space=pl.ANY), vmem, vmem, vmem],
        out_specs=vmem,
        out_shape=jax.ShapeDtypeStruct((2, rank, depth), F32),
        scratch_shapes=[pltpu.VMEM((rank, rank), F32)] + stream_scratch(depth, tile, 2 * (size // tile)),
        compiler_params=params(VMEM_REST),
        cost_estimate=pl.CostEstimate(
            flops=4 * rank * depth * size, bytes_accessed=4 * depth * size, transcendentals=0
        ),
        name="second_pass",
    )(token, w, b, a, cd)


def join_kernel(share, order, nx, nc, me_ref, *refs):
    x_refs, seconds, ut_refs = refs[:nx], refs[nx : nx + nc], refs[nx + nc : -(nx + 2)]
    outs, (x_all, total) = refs[-(nx + 2) : -2], refs[-2:]
    me, row = me_ref[0], me_ref[1]
    place_tokens(order, share, me, row, x_refs, x_all)
    rank = total.shape[0] // 2
    x = x_all[...]
    for p in range(2):
        ut = ut_refs[0][:, p * rank : (p + 1) * rank].astype(BF)
        away = seconds[0][p]
        for second in seconds[1:]:
            away = away + second[p]
        total[p * rank : (p + 1) * rank, :] = dot(ut, x, ((0,), (0,))) - away
    piece = 2 * rank // nx
    for k in range(nx):
        start = pl.multiple_of((row ^ k) * piece, piece)
        outs[k][...] = total[pl.ds(start, piece), :].astype(outs[k].dtype)


def join_call(share, order, me, xs, seconds, uts):
    depth = xs[0].shape[1]
    rank = seconds[0].shape[1]
    nx = len(xs)
    rows = sum(x.shape[0] for x in xs)
    piece = 2 * rank // nx
    vmem = pl.BlockSpec(memory_space=pltpu.VMEM)
    return pl.pallas_call(
        functools.partial(join_kernel, share, order, nx, len(seconds)),
        in_specs=[pl.BlockSpec(memory_space=pltpu.SMEM)] + [vmem] * (nx + len(seconds) + len(uts)),
        out_specs=[vmem] * nx,
        out_shape=[jax.ShapeDtypeStruct((piece, depth), F32 if k == 0 else BF) for k in range(nx)],
        scratch_shapes=[pltpu.VMEM((rows, depth), BF), pltpu.VMEM((2 * rank, depth), F32)],
        compiler_params=params(VMEM_REST),
        name="join_grad_in",
    )(me, *xs, *seconds, *uts)


def lay_kernel(me_ref, *refs):
    out_ref = refs[-1]
    row = me_ref[1]
    for k, ref in enumerate(refs[:-1]):
        piece = ref.shape[0]
        start = pl.multiple_of((row ^ k) * piece, piece)
        out_ref[pl.ds(start, piece), :] = ref[...].astype(F32)


def lay_call(me, pieces):
    rows = sum(x.shape[0] for x in pieces)
    vmem = pl.BlockSpec(memory_space=pltpu.VMEM)
    return pl.pallas_call(
        lay_kernel,
        in_specs=[pl.BlockSpec(memory_space=pltpu.SMEM)] + [vmem] * len(pieces),
        out_specs=vmem,
        out_shape=jax.ShapeDtypeStruct((rows, pieces[0].shape[1]), F32),
        compiler_params=params(VMEM_REST),
        name="lay_grad_in",
    )(me, *pieces)


def fold_kernel(n, orders, *refs):
    (ad_keep, ad_got, g_keep, g_got, sq_ref, stat_ref, mag_ref), outs = refs[:7], refs[7:]
    cd_ref, blocks = outs[0], outs[1:]
    rows = g_keep.shape[1] * 2 // n
    totals = []
    for p in range(2):
        inverse = lax.rsqrt(sq_ref[p] + EPSILON)
        coef = mag_ref[p] * inverse
        cd = coef * stat_ref[p] * (inverse * inverse)
        cd_ref[p] = cd
        g = g_keep[p].astype(F32) + g_got[p].astype(F32)
        ad = ad_keep[p].astype(F32) + ad_got[p].astype(F32)
        totals.append(coef * g - cd * ad)
    for i, j in enumerate(range(0, n, 2)):
        at = [block_at(n, order).index(j) * rows for order in orders]
        both = [totals[p][at[p] : at[p] + rows] for p in range(2)]
        blocks[i][...] = jnp.concatenate(both, axis=0).astype(blocks[i].dtype)


def fold_call(n, orders, ad_keep, ad_got, g_keep, g_got, sq, stat, mag):
    _, half, width = ad_keep.shape
    tile = tile_of(width, 3584)
    rows = half * 4 // n
    big = pl.BlockSpec((2, half, tile), lambda f: (0, 0, f))
    line = pl.BlockSpec((2, 1, tile), lambda f: (0, 0, f))
    return pl.pallas_call(
        functools.partial(fold_kernel, n, orders),
        grid=(width // tile,),
        in_specs=[big] * 4 + [line] * 3,
        out_specs=[line] + [pl.BlockSpec((rows, tile), lambda f: (0, f))] * (n // 2),
        out_shape=[jax.ShapeDtypeStruct((2, 1, width), F32)]
        + [jax.ShapeDtypeStruct((rows, width), F32 if j == 0 else BF) for j in range(n // 2)],
        compiler_params=params(VMEM_REST),
        name="fold_rows",
    )(ad_keep, ad_got, g_keep, g_got, sq, stat, mag)


def order_kernel(n, orders, has_prior, me_ref, low_ref, high_ref, *refs):
    out_ref = refs[-1]
    rank = out_ref.shape[1]
    for p in range(2):
        choice = row_choice(n, rank // n, me_ref[0], orders[p], transpose=True)
        both = jnp.concatenate([low_ref[p], high_ref[p]], axis=0)
        out_ref[p] = dot(choice, both)


def order_call(n, orders, me, low, high, prior, first, width):
    _, half, size = low.shape
    tile = tile_of(math.gcd(first, size), 3584)
    start = first // tile
    args = [me, low, high]
    specs = [
        pl.BlockSpec(memory_space=pltpu.SMEM),
        pl.BlockSpec((2, half, tile), lambda f: (0, 0, f)),
        pl.BlockSpec((2, half, tile), lambda f: (0, 0, f)),
    ]
    aliases = {}
    if prior is not None:
        aliases = {3: 0}
        args.append(prior)
        specs.append(pl.BlockSpec(memory_space=pl.ANY))
    return pl.pallas_call(
        functools.partial(order_kernel, n, orders, prior is not None),
        grid=(size // tile,),
        in_specs=specs,
        out_specs=pl.BlockSpec((2, 2 * half, tile), lambda f: (0, 0, f + start)),
        out_shape=jax.ShapeDtypeStruct((2, 2 * half, width), F32),
        input_output_aliases=aliases,
        compiler_params=params(VMEM_REST),
        name="order_rows",
    )(*args)


def tied(*xs):
    return lax.optimization_barrier(xs)


class Turn:
    def __init__(self, token):
        self.token = token

    def pass_on(self, *xs):
        self.token, *xs = tied(self.token, *xs)
        return tuple(xs)


class Halving:
    def __init__(self, orders, keep, send, dtype=BF):
        self.flat = keep.ndim == 2
        self.orders, self.dtype = orders[:1] if self.flat else orders, dtype
        self.parts = [(keep,) if self.flat else (keep[0], keep[1])]
        self.whole = [keep]
        self.send, self.step, self.rows = [send], 0, keep.shape[0 if self.flat else 1]

    def sums(self, low, high):
        return [sum(part[p][low:high].astype(F32) for part in self.parts) for p in range(len(self.orders))]

    def prepare(self):
        if self.step:
            self.rows //= 2
            self.send = [x.astype(self.dtype) for x in self.sums(self.rows, 2 * self.rows)]
        return self.send

    def go(self, send):
        if self.step:
            self.got = [swap(x, "col", order[self.step]) for x, order in zip(send, self.orders)]
        else:
            self.got = [swap(send[0], "col", self.orders[0][0])]
        return self.got

    def arrived(self, got):
        if self.step or self.flat:
            self.parts.append(tuple(got))
            self.whole.append(tuple(got) if len(got) > 1 else got[0])
        else:
            self.parts.append((got[0][0], got[0][1]))
            self.whole.append(got[0])
        self.step += 1

    def done(self):
        return self.step == len(self.orders[0])

    def own(self):
        return self.sums(0, self.rows)

    def pairs(self):
        return [x if isinstance(x, tuple) else (x, x) for x in self.whole]


class Lanes:
    def __init__(self, bits, squares, xa):
        self.bits, self.squares, self.xa = bits, squares, xa

    def prepare(self):
        return [jnp.concatenate([self.squares, *self.xa.prepare()], axis=0)]

    def go(self, send):
        return [swap(send[0], "col", self.bits[self.xa.step])]

    def arrived(self, got):
        rows = self.squares.shape[0]
        self.squares = self.squares + got[0][:rows]
        self.xa.arrived([got[0][rows:]])

    def done(self):
        return self.xa.done()


class Statistic:
    def __init__(self, n, stat, u):
        self.n, self.stat, self.u, self.step = n, stat, u, 0

    def prepare(self):
        both = jnp.concatenate([self.stat, self.u], axis=0)
        return [both.astype(BF) if self.step else both]

    def go(self, send):
        return [swap(send[0], "col", j) for j in ([1], range(2, self.n, 2))[self.step]]

    def arrived(self, got):
        rows = self.stat.shape[0]
        self.stat = self.stat + sum(x[:rows].astype(F32) for x in got)
        self.u = jnp.concatenate([self.u] + [x[rows:].astype(F32) for x in got], axis=0)
        self.step += 1

    def done(self):
        return self.step == 2


class First:
    def __init__(self, send):
        self.send, self.got = send, None

    def prepare(self):
        return [self.send]

    def go(self, send):
        return [swap(send[0], "col", 1)]

    def arrived(self, got):
        self.got = got[0]

    def done(self):
        return self.got is not None


class Scattering:
    def __init__(self, n, blocks):
        self.n, self.blocks, self.own = n, blocks, None

    def prepare(self):
        return self.blocks[1:]

    def go(self, send):
        return [swap(x, "col", j) for x, j in zip(send, range(2, self.n, 2))]

    def arrived(self, got):
        total = sum(x.astype(F32) for x in [self.blocks[0], *got])
        rows = total.shape[0] // 2
        self.own = [total[p * rows : (p + 1) * rows].astype(BF) for p in range(2)]

    def done(self):
        return self.own is not None


class Laying:
    def __init__(self, orders, own):
        self.orders, self.held, self.step = orders, own, len(orders[0]) - 1

    def prepare(self):
        return self.held if self.step else [jnp.stack(self.held)]

    def go(self, send):
        self.held = list(send)
        if self.step:
            return [swap(x, "col", order[self.step]) for x, order in zip(send, self.orders)]
        return [swap(send[0], "col", self.orders[0][0])]

    def arrived(self, got):
        if self.step:
            self.held = [jnp.concatenate(pair, axis=0) for pair in zip(self.held, got)]
        else:
            self.held += list(got)
        self.step -= 1

    def done(self):
        return self.step < 0


class Around:
    def __init__(self, n, xs):
        self.n, self.xs, self.got = n, xs, None

    def prepare(self):
        return self.xs

    def go(self, send):
        return [swap(x, "row", k) for k, x in enumerate(send, start=1)]

    def arrived(self, got):
        self.got = list(got)

    def done(self):
        return self.got is not None


def phase(turn, moves, kernel=None, late=(), ready=()):
    moves = [move for move in moves if not move.done()]
    late = [move for move in late if not move.done()]
    ready = [move for move in ready if not move.done()]
    sends = [move.prepare() for move in moves + late]
    sent = list(turn.pass_on(*[x for send in sends for x in send]))
    got = [move.go([sent.pop(0) for _ in send]) for move, send in zip(moves + late, sends)]
    for move, g in zip(late, got[len(moves) :]):
        move.pending = g
    waited = moves + ready
    got = got[: len(moves)] + [move.pending for move in ready]
    outs = kernel(turn.token) if kernel else ()
    flat = list(turn.pass_on(*[x for g in got for x in g], *outs))
    for move, g in zip(waited, got):
        move.arrived([flat.pop(0) for _ in g])
    return flat


def on_device(tokens, weights, adapter_in, adapter_out, magnitude, hidden_cot):
    n, n_row = lax.axis_size("col"), lax.axis_size("row")
    rank = adapter_in.shape[1]
    share = hidden_cot.shape[0]
    width = weights.shape[2]
    orders = bit_orders(n)
    bits = orders[0]
    steps = len(bits)
    me = jnp.stack([lax.axis_index("col"), lax.axis_index("row")]).astype(jnp.int32)
    mag = magnitude[:, None, :]
    sizes = [width * q // sum(QUARTERS) for q in QUARTERS]
    firsts = [sum(sizes[:c]) for c in range(len(sizes))]
    count = len(sizes)

    xs = [tokens] + [swap(tokens, "row", k) for k in range(1, n_row)]
    ad_keep, ad_send, sq = adapter_call(n, orders, me, adapter_in, weights, adapter_out)
    turn = Turn(me)
    *xs, sq, ad_send = turn.pass_on(*xs, sq, ad_send)
    sq_first, ad_first = First(sq.reshape(-1, 128)), First(ad_send)

    def project(c):
        return lambda token: token_call(
            n, share, orders, token, xs, adapter_in, weights, adapter_out, firsts[c], sizes[c], c == 0
        )

    def elementwise(c):
        return lambda token: own_call(
            n, orders, token, share, halvings[c].pairs(), [x[0] for x in xa.parts], squares, mag, adapter_out,
            hidden_cot, hidden, firsts[c], sizes[c],
        )

    outs = phase(turn, [sq_first, ad_first], project(0))
    halvings = [Halving(orders, outs[0], outs[1])]
    xa = Halving(orders, outs[2], outs[3], F32)
    phase(turn, [xa, halvings[0]])
    lanes = Lanes(bits, sq_first.send + sq_first.got, xa)
    for c in range(1, count):
        outs = phase(turn, [lanes, halvings[c - 1]], project(c))
        halvings.append(Halving(orders, outs[0], outs[1]))
        phase(turn, halvings)
        phase(turn, [lanes, halvings[-1]])
    hidden, results = None, []
    for c in range(count):
        while not (lanes.done() and halvings[c].done()):
            phase(turn, [lanes, halvings[c]])
        squares = lanes.squares.reshape(2, 1, -1)
        hidden, *outs = phase(turn, halvings[c + 1 : c + 2], elementwise(c))
        results.append(outs)
    g_keep, g_send = [jnp.concatenate([r[i] for r in results], axis=2) for i in range(2)]
    g_first = First(g_send)
    stat = jnp.concatenate([r[2] for r in results], axis=2).reshape(-1, 128)
    statistic = Statistic(n, stat, sum(r[3] for r in results))
    phase(turn, [statistic, g_first])
    phase(turn, [statistic])
    stat = statistic.stat.reshape(2, 1, -1)
    cd, *blocks = fold_call(n, orders, ad_keep, ad_first.got, g_keep, g_first.got, squares, stat, mag)
    scattering = Scattering(n, blocks)
    seconds = phase(
        turn,
        [scattering],
        lambda token: [second_call(weights, adapter_out, adapter_in, cd, 0, width, token)],
    )
    laying = Laying(orders, scattering.own)
    pieces = turn.pass_on(*join_call(share, bits[::-1], turn.token, xs, seconds, [statistic.u]))
    away = Around(n_row, pieces[1:])
    phase(turn, [laying, away])
    total = (pieces[0] + sum(x.astype(F32) for x in away.got)).astype(BF)
    back = Around(n_row, [total] * (n_row - 1))
    while laying.step or not back.done():
        phase(turn, [laying, back])
    (grad_in,) = phase(turn, [laying], lambda token: [lay_call(token, [total] + back.got)])
    low, high = laying.held
    grad_out = order_call(n, orders, turn.token, low, high, None, 0, width)
    grad_in = grad_in.reshape(2, -1, grad_in.shape[1])
    grad_mag = (stat / jnp.sqrt(squares + EPSILON))[:, 0, :]
    return (hidden, grad_in, grad_out, grad_mag)


def solution(mesh):
    in_specs = (
        P("row", "col"),
        P(None, "col", "row"),
        P(None, None, "col"),
        P(None, None, "row"),
        P(None, "row"),
        P("col", "row"),
    )
    out_specs = (P("col", "row"), P(None, None, "col"), P(None, None, "row"), P(None, "row"))
    return jax.shard_map(
        on_device, mesh=mesh, in_specs=in_specs, out_specs=out_specs, check_vma=False
    )
```
